256 devices in a mesh: scene: 8 (over z_lo, core), row: 8 (over x, z_hi), col: 4 (over y).
Axes of the slice: x: 4, y: 4, z: 8 (z_hi: 2, z_lo: 4; z = z_hi * 4 + z_lo), core: 2. Of those that a mesh axis runs over, the one named last changes fastest.
Arguments:
- scene: bfloat16 [1024, 256, 768], P(('scene', 'row'), 'col'), parts along dimension 0, may hold values from -6 to 6
- cotangent: bfloat16 [1024, 256, 768], P(('scene', 'row'), 'col'), parts along dimension 0, may hold values from -6 to 6
- query_key_value_weight: bfloat16 [768, 2304], replicated
- proj_weight: bfloat16 [768, 768], replicated, may hold values from -0.21875 to 0.21875
- kept: int32 [256, 16], P('scene'), parts along dimension 0, may hold values from 0 to 1, as said below
Outputs:
- scene_grad: bfloat16 [1024, 256, 768], P(('scene', 'row'), 'col'), parts along dimension 0
- qkv_grad: float32 [6144, 2304], P(('scene', 'row', 'col')), parts along dimension 0
- proj_grad: float32 [6144, 768], P(('scene', 'row', 'col')), parts along dimension 0
The draws below stay inside these ranges and needn't reach their ends.
There are 8 independent parts, one for each index of `scene`. The reference program is written for one: setup_inputs(seed, part) draws one part's arguments, and reference() takes and returns one part's arrays. A program takes and returns all parts, laid end to end along the dimension named above; an argument that names none is the same for every part. Nothing has to cross between parts.
Inputs may be any that keep to these rules, and one draw needn't show every extreme that they name: Within each column of tiles (same second device-grid index) exactly 48 windows are kept; no tile keeps more than 12 windows and in every column of tiles some tile keeps exactly 12.
All inputs are finite; a program needn't handle non-finite values.
Results may differ from the reference program's by a relative error of at most 0.0085.
Values may be sent and summed in bfloat16 or wider, within the bound.
A program may use at most 128 MiB of HBM per device.

```python
import jax
import jax.numpy as jnp
from jax import lax

HD = 32
D = 768
WIN = 8
TR = 16
TC = 64
KEEP_DEV = 6
HEIGHT = 128
WIDTH = 256
WT = 16
N_ROW = 8
N_COL = 4


def draw_query_key_value_weight(key, part):
    key = jax.random.fold_in(key, 23)
    first = jax.random.fold_in(key, 0)
    weight = jax.random.normal(first, (D, 3 * D), jnp.float32) * D ** (-0.5)
    return weight.astype(jnp.bfloat16)


def draw_kept(key, part):
    key = jax.random.fold_in(key, 11)
    first, second, third = jax.random.split(key, 3)
    order = jax.vmap(lambda k: jax.random.permutation(k, N_ROW))(jax.random.split(first, N_COL))
    spread = jax.random.randint(second, (N_COL, N_ROW // 2), 0, KEEP_DEV + 1)
    spread = spread.at[:, 0].set(KEEP_DEV)
    delta = jnp.stack([spread, -spread], axis=-1).reshape(N_COL, N_ROW)
    col_index = jnp.broadcast_to(jnp.arange(N_COL)[:, None], (N_COL, N_ROW))
    counts = jnp.zeros((N_COL, N_ROW), jnp.int32).at[col_index, order].set(KEEP_DEV + delta)
    counts = counts.T.reshape(N_ROW * N_COL)
    places = jax.vmap(lambda k: jax.random.permutation(k, WT))(jax.random.split(third, N_ROW * N_COL))
    return (places < counts[:, None]).astype(jnp.int32)


def spiked(result, stream_key, source, target, shards_of, factor):
    def block_of(axis_at):
        return (jnp.arange(result.shape[axis_at]) // (result.shape[axis_at] // shards_of)).reshape((-1,) + (1,) * (result.ndim - 1 - axis_at))

    one_side = jax.random.permutation(stream_key, shards_of)[block_of(target)]
    second = (block_of(target) + shards_of // 2) % shards_of
    return jnp.where((block_of(source) == one_side) | (block_of(source) == second), factor * result, result)


def block_scale(key, extent, cuts, least, high):
    factor_of, own = 1.0, jax.random.fold_in(key, 6)
    for position, blocks in cuts:
        draws = jnp.exp(jax.random.uniform(jax.random.fold_in(own, position), (blocks,), jnp.float32, least / len(cuts), high / len(cuts)))
        factor_of = factor_of * jnp.repeat(draws, extent[position] // blocks).reshape([-1 if axis == position else 1 for axis in range(len(extent))])
    return factor_of


def scatter_about(stream_key, dims, scale, bound, cuts=(), held_as=jnp.bfloat16):
    gain = block_scale(stream_key, dims, cuts, -0.22, 0.18) if cuts else 1.0
    entries = jax.random.normal(stream_key, dims, jnp.float32) * scale * gain
    return jnp.minimum(jnp.maximum(entries, -bound), bound).astype(held_as)


def gaussian_with(own_key, dims, scale, bound, cuts, heavy, kind=jnp.bfloat16):
    values = scale * jax.random.normal(own_key, dims, jnp.float32)
    if cuts:
        values = values * block_scale(own_key, dims, cuts, -0.22, 0.18)
    return jnp.clip(spiked(values, jax.random.fold_in(own_key, 3), *heavy), -bound, bound).astype(kind)


def setup_inputs(seed: int = 0, part: int = 0) -> dict:
    arg_keys = jax.random.split(jax.random.key(seed), 6)
    part_splits = jax.random.split(jax.random.fold_in(arg_keys[5], part), 6)
    return {
        "scene": scatter_about(part_splits[0], (HEIGHT, WIDTH, D), 1.0, 6.0, ((0, 8), (1, 4))),
        "cotangent": gaussian_with(part_splits[1], (HEIGHT, WIDTH, D), 1.0, 6.0, ((0, 8), (1, 4)), (0, 2, 8, 2.0)),
        "query_key_value_weight": draw_query_key_value_weight(jax.random.fold_in(arg_keys[5], 71), part),
        "proj_weight": scatter_about(arg_keys[3], (D, D), D ** -0.5, 0.21875),
        "kept": draw_kept(jax.random.fold_in(jax.random.fold_in(arg_keys[5], part), 71), part),
    }


def window_bias(grow, gcol, height, span):
    offs = jnp.arange(WIN, dtype=jnp.int32)
    rows = grow[:, None] * WIN + offs[None, :]
    cols = gcol[:, None] * WIN + offs[None, :]
    row_label = (rows >= height - WIN).astype(jnp.int32) + (rows >= height - WIN // 2).astype(jnp.int32)
    col_label = (cols >= span - WIN).astype(jnp.int32) + (cols >= span - WIN // 2).astype(jnp.int32)
    label = (3 * row_label[:, :, None] + col_label[:, None, :]).reshape(grow.shape[0], WIN * WIN)
    same = label[:, :, None] == label[:, None, :]
    return jnp.where(same, 0.0, -100.0).astype(jnp.float32)

def window_grads(xw, gw, query_key_value_weight, proj_weight, bias):
    count, area, width = xw.shape
    heads = width // HD
    single_precision = jnp.float32
    xf = xw.astype(single_precision)
    input_mean = lax.optimization_barrier(jnp.mean(xf, axis=-1, keepdims=True))
    centered_input = xf - input_mean
    inverse_deviation = lax.rsqrt(lax.optimization_barrier(jnp.mean(centered_input * centered_input, axis=-1, keepdims=True)) + 1e-05)
    normed_input = centered_input * inverse_deviation
    input_block = normed_input.astype(jnp.bfloat16)
    query_weight = query_key_value_weight.astype(single_precision)
    wp = proj_weight.astype(single_precision)
    qkv = jnp.einsum('nsd,de->nse', input_block.astype(single_precision), query_weight).astype(jnp.bfloat16)
    query = qkv[:, :, :width].reshape(count, area, heads, HD).astype(single_precision)
    keys = qkv[:, :, width:2 * width].reshape(count, area, heads, HD).astype(single_precision)
    values = qkv[:, :, 2 * width:].reshape(count, area, heads, HD).astype(single_precision)
    scale = HD ** (-0.5)
    scores = jnp.einsum('nqhc,nkhc->nhqk', query, keys) * scale + bias[:, None]
    top = lax.optimization_barrier(jnp.max(scores, axis=-1, keepdims=True))
    expo = jnp.exp(scores - top)
    probs = expo / lax.optimization_barrier(jnp.sum(expo, axis=-1, keepdims=True))
    pb = probs.astype(jnp.bfloat16).astype(single_precision)
    attended = jnp.einsum('nhqk,nkhc->nqhc', pb, values).reshape(count, area, width).astype(jnp.bfloat16)
    gf = gw.astype(single_precision)
    d_att = jnp.einsum('jkp,wp->jkw', gf, wp).astype(jnp.bfloat16)
    proj_part = jnp.einsum('nsd,nse->de', attended.astype(single_precision), gf)
    d_heads = d_att.reshape(count, area, heads, HD).astype(single_precision)
    d_p = jnp.einsum('nqhc,nkhc->nhqk', d_heads, values)
    d_v = jnp.einsum('nhqk,nqhc->nkhc', pb, d_heads).astype(jnp.bfloat16)
    d_s = (probs * (d_p - lax.optimization_barrier(jnp.sum(probs * d_p, axis=-1, keepdims=True))) * scale).astype(jnp.bfloat16).astype(single_precision)
    d_q = jnp.einsum('nhqk,nkhc->nqhc', d_s, keys).astype(jnp.bfloat16)
    d_k = jnp.einsum('nhqk,nqhc->nkhc', d_s, query).astype(jnp.bfloat16)
    projected_gradient = jnp.concatenate([d_q.reshape(count, area, width), d_k.reshape(count, area, width), d_v.reshape(count, area, width)], axis=-1)
    query_gradient_full = projected_gradient.astype(single_precision)
    qkv_part = jnp.einsum('nsd,nse->de', input_block.astype(single_precision), query_gradient_full)
    normed_gradient = jnp.einsum('jkp,wp->jkw', query_gradient_full, query_weight)
    branch_index = inverse_deviation * (normed_gradient - lax.optimization_barrier(jnp.mean(normed_gradient, axis=-1, keepdims=True)) - normed_input * lax.optimization_barrier(jnp.mean(normed_gradient * normed_input, axis=-1, keepdims=True)))
    return (branch_index.astype(jnp.bfloat16), qkv_part, proj_part)

def reference(scene, cotangent, query_key_value_weight, proj_weight, kept):
    height = TR * N_ROW
    span = TC * N_COL
    wrows = height // WIN
    wcols = span // WIN
    width = scene.shape[2]
    half = WIN // 2
    rolled = jnp.roll(scene, (-half, -half), (0, 1))
    rolled_grad = jnp.roll(cotangent, (-half, -half), (0, 1))

    def to_windows(field):
        return field.reshape(wrows, WIN, wcols, WIN, width).transpose(0, 2, 1, 3, 4).reshape(wrows * wcols, WIN * WIN, width)
    xwin = to_windows(rolled)
    gwin = to_windows(rolled_grad)
    flags = kept.reshape(N_ROW, N_COL, TR // WIN, TC // WIN).transpose(0, 2, 1, 3).reshape(-1)
    total = KEEP_DEV * N_ROW * N_COL
    chosen = jnp.nonzero(flags, size=total)[0].astype(jnp.int32)
    groups = chosen.reshape(total // KEEP_DEV, KEEP_DEV)

    def step(carry, index):
        bias = window_bias(index // wcols, index % wcols, height, span)
        dxw, qkv_part, proj_part = window_grads(xwin[index], gwin[index], query_key_value_weight, proj_weight, bias)
        return ((carry[0] + qkv_part, carry[1] + proj_part), dxw)
    start = (jnp.zeros(query_key_value_weight.shape, jnp.float32), jnp.zeros(proj_weight.shape, jnp.float32))
    sums, pieces = lax.scan(step, start, groups)
    branch_index = jnp.zeros((wrows * wcols, WIN * WIN, width), jnp.bfloat16).at[chosen].set(pieces.reshape(total, WIN * WIN, width))
    branch_index = branch_index.reshape(wrows, wcols, WIN, WIN, width).transpose(0, 2, 1, 3, 4).reshape(height, span, width)
    branch_index = jnp.roll(branch_index, (half, half), (0, 1))
    scene_grad = (cotangent.astype(jnp.float32) + branch_index.astype(jnp.float32)).astype(jnp.bfloat16)
    return (scene_grad, sums[0], sums[1])
```

```python
import functools

import jax
import jax.numpy as jnp
from jax import lax
from jax.experimental import pallas as pl
from jax.experimental.pallas import tpu as pltpu
from jax.sharding import PartitionSpec as P

HD = 32
WIN = 8
HALF = 4
AREA = 64
PACK = 4
GROUP = PACK * HD
BATCH = 4 * AREA
F32 = jnp.float32
BF16 = jnp.bfloat16
NT = (((1,), (1,)), ((), ()))
TN = (((0,), (0,)), ((), ()))


def dot(a, b, dims=(((1,), (0,)), ((), ()))):
    return lax.dot_general(a, b, dims, preferred_element_type=F32)


def swap_halves(tile):
    return pltpu.roll(tile, HALF, tile.ndim - 2)


def kernel(names, *refs):
    r = dict(zip(names, refs))
    scene, cot = r["scene"], r["cotangent"]
    xg, br, stash_d, stash_g = r["xg"], r["br"], r["stash_d"], r["stash_g"]
    stash_xt, stash_at = r["stash_xt"], r["stash_at"]
    xb_s, xh_s, inv_s, qkv_s, dat_s, att_s = (
        r["xb"], r["xh"], r["inv"], r["qkv"], r["dat"], r["att"],
    )
    wqkv, wp = r["wqkv"], r["wp"]
    tile_rows, tile_cols, width = scene.shape
    groups = width // GROUP
    row, col = lax.axis_index("row"), lax.axis_index("col")
    nrow, ncol = lax.axis_size("row"), lax.axis_size("col")
    x_at, z_at = row // 2, row % 2
    myself = row * ncol + col

    def at(drow, dcol):
        return {"row": (row + drow + nrow) % nrow, "col": (col + dcol + ncol) % ncol}

    def send(number, src, dst, device):
        return pltpu.make_async_remote_copy(
            src_ref=src,
            dst_ref=dst,
            send_sem=r["send_sems"].at[number],
            recv_sem=r["recv_sems"].at[number],
            device_id=device,
            device_id_type=pl.DeviceIdType.MESH,
        )

    own = pl.ds(0, tile_rows)
    loads = [
        pltpu.make_async_copy(src, dst, r["load_sems"].at[k])
        for k, (src, dst) in enumerate(
            [
                (scene, xg.at[0, own, pl.ds(0, tile_cols)]),
                (cot, xg.at[1, own, pl.ds(0, tile_cols)]),
                (r["wqkv_hbm"], wqkv),
                (r["wp_hbm"], wp),
            ]
        )
    ]
    for load in loads:
        load.start()

    z_across = 1 - 2 * z_at
    partners = [(-1, 0), (1, 0), (0, -1), (0, 1), (-1, -1), (1, 1), (2, 0), (-2, 0)]
    barrier = pltpu.get_barrier_semaphore()
    for partner in partners:
        pl.semaphore_signal(
            barrier, inc=1, device_id=at(*partner), device_id_type=pl.DeviceIdType.MESH
        )
    pl.semaphore_wait(barrier, len(partners))

    def row_halo(array, half):
        src = (scene, cot)[array]
        columns = pl.ds(half * 2 * 16, 2 * 16)
        return send(
            2 * half + array,
            src.at[pl.ds(0, HALF), columns],
            xg.at[array, pl.ds(tile_rows, HALF), columns],
            at(-1, 0),
        )

    for half in (1, 0):
        for array in (0, 1):
            row_halo(array, half).start()

    low = lax.broadcasted_iota(jnp.int32, (WIN, width), 0) < HALF

    loads[0].wait()
    loads[1].wait()

    def pack_columns(k, _):
        for array in (0, 1):
            pair = xg[array, pl.ds(2 * k, 2), pl.ds(0, 16)].astype(F32)[:, :WIN]
            tile = jnp.where(low, pair[0], swap_halves(pair[1]))
            r["edge_f"][array, pl.ds(pl.multiple_of(k * WIN, WIN), WIN)] = tile
        return 0

    lax.fori_loop(0, tile_rows // 2, pack_columns, 0)
    r["edge_out"][...] = r["edge_f"][...].astype(BF16)

    edge_in = r["edge_in"]
    tokens = tile_rows * HALF
    col_halo = send(
        4,
        r["edge_out"].at[:, pl.ds(16, tokens - 16)],
        edge_in.at[:, pl.ds(0, tokens - 16)],
        at(0, -1),
    )
    corner = send(
        5, r["edge_out"].at[:, pl.ds(0, 16)], edge_in.at[:, pl.ds(tokens - 16, 16)], at(-1, -1)
    )
    col_halo.start()
    corner.start()

    def unpack_columns(first, count):
        def body(k, _):
            for array in (0, 1):
                both = edge_in[array, pl.ds(pl.multiple_of(k * 16, 16), 16)].astype(F32)
                for n in (0, 1):
                    tile = both[n * WIN : (n + 1) * WIN]
                    for odd in (0, 1):
                        part = swap_halves(tile) if odd else tile
                        whole = jnp.concatenate([part, jnp.zeros_like(part)], axis=0)
                        xg[array, HALF + 4 * k + 2 * n + odd, pl.ds(tile_cols, 16)] = whole.astype(
                            BF16
                        )
            return 0

        lax.fori_loop(first, first + count, body, 0)

    for load in loads[2:]:
        load.wait()

    edge_ret, left_in = r["edge_ret"], r["left_in"]
    col_back = send(
        6, edge_ret.at[pl.ds(0, tokens - 16)], left_in.at[pl.ds(16, tokens - 16)], at(0, 1)
    )
    corner_back = send(
        7, edge_ret.at[pl.ds(tokens - 16, 16)], left_in.at[pl.ds(0, 16)], at(1, 1)
    )

    def row_back(half):
        columns = pl.ds(half * 2 * 16, 2 * 16)
        return send(
            8 + half,
            br.at[pl.ds(tile_rows, HALF), columns],
            br.at[pl.ds(0, HALF), columns],
            at(1, 0),
        )

    scale = HD ** (-0.5)
    lane_head = lax.broadcasted_iota(jnp.int32, (AREA, GROUP), 1) // HD
    key_at = lax.broadcasted_iota(jnp.int32, (AREA, PACK * AREA), 0)
    query_at = lax.broadcasted_iota(jnp.int32, (AREA, PACK * AREA), 1) % AREA
    row_differs = jnp.where(key_at // 32 != query_at // 32, 1, 0)
    col_differs = jnp.where((key_at % 8) // 4 != (query_at % 8) // 4, 1, 0)

    def spread(block):
        zero = jnp.zeros_like(block)
        return jnp.concatenate([jnp.where(lane_head == h, block, zero) for h in range(PACK)], axis=0)

    def gather_heads(full):
        total = full[:AREA]
        for h in range(1, PACK):
            total = jnp.where(lane_head == h, full[h * AREA : (h + 1) * AREA], total)
        return total

    def batch(b, _):
        i = b // 2
        half = (b % 2 + b // 2) % 2

        @pl.when(b == 1)
        def _():
            col_halo.wait_recv()
            unpack_columns(0, (tile_rows - HALF) // 4)

        @pl.when(b == 2)
        def _():
            row_halo(0, 1).wait_recv()
            row_halo(1, 1).wait_recv()
            corner.wait_recv()
            unpack_columns((tile_rows - HALF) // 4, 1)

        @pl.when(b == 3)
        def _():
            row_halo(0, 0).wait_recv()
            row_halo(1, 0).wait_recv()

        first = pl.multiple_of(b * BATCH, BATCH)

        def normalise(n, _):
            pair, rows = n // 4, n % 4
            m = 2 * half + pair
            top = WIN * i + HALF + 2 * rows
            here = pl.ds(pl.multiple_of(16 * m, 16), 16)
            following = pl.ds(pl.multiple_of(16 * m + 16, 16), 16)
            for array in (0, 1):
                t0 = xg[array, pl.ds(top, 2), here].astype(F32)
                t1 = xg[array, pl.ds(top, 2), following].astype(F32)
                lo, hi, nx = t0[:, :WIN], t0[:, WIN:], t1[:, :WIN]
                for w, (a, c) in enumerate(((lo, hi), (hi, nx))):
                    tile = jnp.where(low, c, a).reshape(2 * WIN, width)
                    start = pl.multiple_of((2 * pair + w) * AREA + 16 * rows, 16)
                    if array == 0:
                        mean = jnp.mean(tile, axis=-1, keepdims=True)
                        centred = tile - mean
                        inverse = lax.rsqrt(
                            jnp.mean(centred * centred, axis=-1, keepdims=True) + 1e-05
                        )
                        normed = centred * inverse
                        xh_s[pl.ds(start, 16)] = normed
                        xb_s[pl.ds(start, 16)] = normed.astype(BF16)
                        inv_s[pl.ds(start, 16)] = jnp.broadcast_to(inverse, (16, 128))
                    else:
                        keep = r["kept"][myself, WIN * i + 2 * m + w].astype(F32)
                        stash_g[pl.ds(pl.multiple_of(first + start, 16), 16)] = (
                            tile * keep
                        ).astype(BF16)
            return 0

        lax.fori_loop(0, 8, normalise, 0)
        xb = xb_s[...]
        stash_xt[:, pl.ds(first, BATCH)] = xb.T
        for n in range(3):
            qkv_s[:, n * width : (n + 1) * width] = dot(
                xb, wqkv[:, n * width : (n + 1) * width]
            ).astype(BF16)
        dat_s[...] = dot(stash_g[pl.ds(first, BATCH)], wp[...], NT).astype(BF16)

        def attend(w, _):
            j = 4 * half + w
            last_row = jnp.where(row == nrow - 1, i, 0)
            last_col = jnp.where(col == ncol - 1, j // 7, 0)
            bias = jnp.where(row_differs * last_row + col_differs * last_col > 0, -100.0, 0.0)
            rows = pl.ds(pl.multiple_of(w * AREA, AREA), AREA)
            out_rows = pl.ds(pl.multiple_of(first + w * AREA, AREA), AREA)
            for g in range(groups):
                lanes = slice(g * GROUP, (g + 1) * GROUP)

                def part(n):
                    return slice(n * width + g * GROUP, n * width + (g + 1) * GROUP)

                q, k, v = qkv_s[rows, part(0)], qkv_s[rows, part(1)], qkv_s[rows, part(2)]
                spread_q, spread_d = spread(q), spread(dat_s[rows, lanes])
                scores = dot(k, spread_q, NT) * scale + bias
                expo = jnp.exp(scores - jnp.max(scores, axis=0, keepdims=True))
                probs = expo * (1.0 / jnp.sum(expo, axis=0, keepdims=True))
                pb = probs.astype(BF16)
                d_p = dot(v, spread_d, NT)
                delta = jnp.sum(probs * d_p, axis=0, keepdims=True)
                d_s = (probs * (d_p - delta) * scale).astype(BF16)
                att_s[rows, lanes] = gather_heads(dot(pb, v, TN)).astype(BF16)
                stash_d[out_rows, part(0)] = gather_heads(dot(d_s, k, TN)).astype(BF16)
                stash_d[out_rows, part(1)] = dot(d_s, spread_q).astype(BF16)
                stash_d[out_rows, part(2)] = dot(pb, spread_d).astype(BF16)
            return 0

        lax.fori_loop(0, 4, attend, 0)
        stash_at[:, pl.ds(first, BATCH)] = att_s[...].T
        r["dxh"][...] = dot(stash_d[pl.ds(first, BATCH)], wqkv[...], NT)

        def finish(n, _):
            pair, at_row = n // WIN, n % WIN
            tiles = []
            for w in (0, 1):
                here = pl.ds(pl.multiple_of((2 * pair + w) * AREA + WIN * at_row, WIN), WIN)
                grad, normed = r["dxh"][here], xh_s[here]
                inverse = inv_s[here][:, :1]
                tiles.append(
                    inverse
                    * (
                        grad
                        - jnp.mean(grad, axis=-1, keepdims=True)
                        - normed * jnp.mean(grad * normed, axis=-1, keepdims=True)
                    )
                )
            where = pl.ds(pl.multiple_of(32 * half + 16 * pair, 16), 16)
            br[HALF + WIN * i + at_row, where] = jnp.concatenate(tiles, axis=0).astype(BF16)
            r["last"][at_row] = tiles[1]
            return 0

        lax.fori_loop(0, 2 * WIN, finish, 0)

        @pl.when(half == 1)
        def _():
            last = r["last"][...]
            packed = [
                jnp.where(low, last[2 * n], swap_halves(last[2 * n + 1])) for n in range(WIN // 2)
            ]
            edge_ret[pl.ds(pl.multiple_of(32 * i, 32), 32)] = jnp.concatenate(
                packed, axis=0
            ).astype(BF16)

        @pl.when(b == 2)
        def _():
            col_back.start()
            corner_back.start()
            row_back(1).start()

        return 0

    lax.fori_loop(0, 4, batch, 0)
    row_back(0).start()

    share = width // (nrow * ncol)
    span = 8 * share

    part_a, part_b = r["part_a"], r["part_b"]

    def grads_a(step):
        target = (x_at + step) % 4
        lhs = stash_xt[pl.ds(pl.multiple_of(target * span, 16), span), :]
        first = dot(lhs, stash_d[:, :width])
        second = dot(lhs, stash_d[:, width : 2 * width])
        for z in range(2):
            for y in range(4):
                rows = slice((4 * z + y) * share, (4 * z + y + 1) * share)
                part_a[target, z, y] = jnp.concatenate([first[rows], second[rows]], axis=0).astype(
                    BF16
                )

    def grads_b(x, _):
        here = pl.ds(pl.multiple_of(x * span, 16), span)
        first = dot(stash_xt[here, :], stash_d[:, 2 * width :])
        second = dot(stash_at[here, :], stash_g[...])
        for z in range(2):
            for y in range(4):
                rows = slice((4 * z + y) * share, (4 * z + y + 1) * share)
                part_b[y, z, x] = jnp.concatenate([first[rows], second[rows]], axis=0).astype(BF16)
        return 0

    class Ring:
        def __init__(self, base, part, me, forward, backward, relay, direct):
            self.part, self.me, self.relay, self.direct = part, me, relay, direct
            ahead, behind, across = (me + 1) % 4, (me + 3) % 4, (me + 2) % 4
            self.ahead, self.behind = ahead, behind
            self.relay_back = send(base, part.at[across, 0], relay.at[0], backward)
            self.relay_on = send(base + 1, part.at[across, 1], relay.at[1], forward)
            self.own_on = send(base + 2, part.at[ahead, 0], direct.at[0, 0], forward)
            self.own_back = send(base + 3, part.at[behind, 1], direct.at[1, 1], backward)
            self.sum_back = send(base + 4, part.at[behind, 0], direct.at[1, 0], backward)
            self.sum_on = send(base + 5, part.at[ahead, 1], direct.at[0, 1], forward)

        def begin(self):
            self.relay_back.start()
            self.relay_on.start()

        def go_on(self):
            self.own_on.start()
            self.own_back.start()

        def pass_on(self):
            for n, copy, relayed, target in (
                (0, self.sum_back, self.relay_back, self.behind),
                (1, self.sum_on, self.relay_on, self.ahead),
            ):
                relayed.wait_recv()
                total = self.part[target, n].astype(F32) + self.relay[n].astype(F32)
                self.part[target, n] = total.astype(BF16)
                copy.start()

        def arrive(self):
            for copy in (self.own_on, self.own_back, self.sum_back, self.sum_on):
                copy.wait_recv()

        def total(self, z):
            return (
                self.part[self.me, z].astype(F32)
                + self.direct[0, z].astype(F32)
                + self.direct[1, z].astype(F32)
            )

        def close(self):
            for copy in (
                self.relay_back, self.relay_on, self.own_on,
                self.own_back, self.sum_back, self.sum_on,
            ):
                copy.wait_send()

    on_x, back_x, on_y, back_y = at(2, 0), at(-2, 0), at(0, 1), at(0, -1)
    next_a, next_b = r["next_a"], r["next_b"]
    ring_a = Ring(10, part_a, x_at, on_x, back_x, r["relay_a"], r["direct_a"])
    ring_b = Ring(16, part_b, col, on_y, back_y, r["relay_b"], r["direct_b"])
    ring_c = Ring(22, next_a, col, on_y, back_y, r["relay_c"], r["direct_c"])
    ring_d = Ring(28, next_b, x_at, on_x, back_x, r["relay_d"], r["direct_d"])

    grads_a(2)
    ring_a.begin()
    lax.fori_loop(0, 4, grads_b, 0)
    ring_b.begin()
    ring_b.go_on()
    grads_a(1)
    grads_a(3)
    ring_a.go_on()
    ring_a.pass_on()
    ring_b.pass_on()
    grads_a(0)

    col_back.wait_recv()
    corner_back.wait_recv()
    row_back(0).wait_recv()
    row_back(1).wait_recv()

    def add_branch(k, _):
        left = left_in[pl.ds(pl.multiple_of(16 * k, 16), 16)].astype(F32)
        for n in range(4):
            at_row = 4 * k + n
            tile = left[WIN * (n // 2) : WIN * (n // 2 + 1)]
            before = swap_halves(tile) if n % 2 else tile
            for m in range(tile_cols // 16):
                here = slice(16 * m, 16 * m + 16)
                both = br[at_row, here].astype(F32)
                lo, hi = both[:WIN], both[WIN:]
                grad = jnp.concatenate(
                    [jnp.where(low, before, lo), jnp.where(low, lo, hi)], axis=0
                )
                before = hi
                r["out"][at_row, here] = (xg[1, at_row, here].astype(F32) + grad).astype(BF16)
        return 0

    lax.fori_loop(0, tile_rows // 4, add_branch, 0)

    ring_a.arrive()
    for z in range(2):
        total = ring_a.total(z).astype(BF16)
        for y in range(4):
            next_a[y, z] = total[y]
    ring_c.begin()
    ring_c.go_on()
    ring_b.arrive()
    for z in range(2):
        total = ring_b.total(z).astype(BF16)
        for x in range(4):
            next_b[x, z] = total[x]
    ring_d.begin()
    ring_d.go_on()
    ring_c.pass_on()
    ring_d.pass_on()

    across = at(z_across, 0)
    last_out, last_in, mine = r["last_out"], r["last_in"], r["mine"]
    crossing = []
    for n, ring in enumerate((ring_c, ring_d)):
        ring.arrive()
        last_out[n] = ring.total(1 - z_at).astype(BF16)
        copy = send(34 + n, last_out.at[n], last_in.at[n], across)
        copy.start()
        crossing.append(copy)
        mine[n] = ring.total(z_at)
    for n, copy in enumerate(crossing):
        copy.wait_recv()
        total = mine[n] + last_in[n].astype(F32)
        if n == 0:
            r["qkv_grad"][:, :width] = total[:share]
            r["qkv_grad"][:, width : 2 * width] = total[share:]
        else:
            r["qkv_grad"][:, 2 * width :] = total[:share]
            r["proj_grad"][...] = total[share:]

    for array in (0, 1):
        for half in (0, 1):
            row_halo(array, half).wait_send()
    for copy in (col_halo, corner, col_back, corner_back, row_back(0), row_back(1), *crossing):
        copy.wait_send()
    for ring in (ring_a, ring_b, ring_c, ring_d):
        ring.close()


def on_device(scene, cotangent, query_key_value_weight, proj_weight, kept):
    rows, cols, width = scene.shape
    share = width // 32
    both = 2 * share
    tokens = rows * HALF
    all_tokens = rows * cols
    vmem = {
        "xg": ((2, rows + HALF, cols + 16, width), BF16),
        "br": ((rows + HALF, cols, width), BF16),
        "stash_d": ((all_tokens, 3 * width), BF16),
        "stash_g": ((all_tokens, width), BF16),
        "stash_xt": ((width, all_tokens), BF16),
        "stash_at": ((width, all_tokens), BF16),
        "xb": ((BATCH, width), BF16),
        "xh": ((BATCH, width), F32),
        "inv": ((BATCH, 128), F32),
        "qkv": ((BATCH, 3 * width), BF16),
        "dat": ((BATCH, width), BF16),
        "att": ((BATCH, width), BF16),
        "dxh": ((BATCH, width), F32),
        "last": ((WIN, WIN, width), F32),
        "wqkv": ((width, 3 * width), BF16),
        "wp": ((width, width), BF16),
        "edge_f": ((2, tokens, width), F32),
        "edge_out": ((2, tokens, width), BF16),
        "edge_in": ((2, tokens, width), BF16),
        "edge_ret": ((tokens, width), BF16),
        "left_in": ((tokens, width), BF16),
        "part_a": ((4, 2, 4, both, width), BF16),
        "part_b": ((4, 2, 4, both, width), BF16),
        "relay_a": ((2, 4, both, width), BF16),
        "relay_b": ((2, 4, both, width), BF16),
        "direct_a": ((2, 2, 4, both, width), BF16),
        "direct_b": ((2, 2, 4, both, width), BF16),
        "next_a": ((4, 2, both, width), BF16),
        "next_b": ((4, 2, both, width), BF16),
        "relay_c": ((2, both, width), BF16),
        "relay_d": ((2, both, width), BF16),
        "direct_c": ((2, 2, both, width), BF16),
        "direct_d": ((2, 2, both, width), BF16),
        "last_out": ((2, both, width), BF16),
        "last_in": ((2, both, width), BF16),
        "mine": ((2, both, width), F32),
    }
    sems = {
        "load_sems": pltpu.SemaphoreType.DMA((4,)),
        "send_sems": pltpu.SemaphoreType.DMA((36,)),
        "recv_sems": pltpu.SemaphoreType.DMA((36,)),
    }
    names = (
        ["scene", "cotangent", "wqkv_hbm", "wp_hbm", "kept", "out", "qkv_grad", "proj_grad"]
        + list(vmem)
        + list(sems)
    )
    anywhere = pl.BlockSpec(memory_space=pl.ANY)
    in_vmem = pl.BlockSpec(memory_space=pltpu.VMEM)
    return pl.pallas_call(
        functools.partial(kernel, names),
        out_shape=(
            jax.ShapeDtypeStruct((rows, cols, width), BF16),
            jax.ShapeDtypeStruct((share, 3 * width), F32),
            jax.ShapeDtypeStruct((share, width), F32),
        ),
        in_specs=[anywhere] * 4 + [pl.BlockSpec(memory_space=pltpu.SMEM)],
        out_specs=(in_vmem,) * 3,
        scratch_shapes=[pltpu.VMEM(*spec) for spec in vmem.values()] + list(sems.values()),
        compiler_params=pltpu.CompilerParams(
            collective_id=0, has_side_effects=True, vmem_limit_bytes=60 * 1024 * 1024
        ),
    )(scene, cotangent, query_key_value_weight, proj_weight, kept)


def solution(mesh):
    return jax.shard_map(
        on_device,
        mesh=mesh,
        in_specs=(
            P(("scene", "row"), "col", None),
            P(("scene", "row"), "col", None),
            P(),
            P(),
            P("scene", None),
        ),
        out_specs=(
            P(("scene", "row"), "col", None),
            P(("scene", "row", "col"), None),
            P(("scene", "row", "col"), None),
        ),
        check_vma=False,
    )
```

```python
import functools

import jax
import jax.numpy as jnp
from jax import lax
from jax.experimental import pallas as pl
from jax.experimental.pallas import tpu as pltpu
from jax.sharding import PartitionSpec as P

HD = 32
WIN = 8
HALF = 4
AREA = 64
PACK = 4
GROUP = PACK * HD
BATCH = 2 * AREA
F32 = jnp.float32
BF16 = jnp.bfloat16
NT = (((1,), (1,)), ((), ()))
TN = (((0,), (0,)), ((), ()))


def dot(a, b, dims=(((1,), (0,)), ((), ()))):
    return lax.dot_general(a, b, dims, preferred_element_type=F32)


def swap_halves(tile):
    return pltpu.roll(tile, HALF, tile.ndim - 2)


def kernel(names, *refs):
    r = dict(zip(names, refs))
    scene, cot = r["scene"], r["cotangent"]
    xg, br, stash_d, stash_g = r["xg"], r["br"], r["stash_d"], r["stash_g"]
    stash_xt, stash_at = r["stash_xt"], r["stash_at"]
    xb_s, xh_s, inv_s, qkv_s, dat_s, att_s = (
        r["xb"], r["xh"], r["inv"], r["qkv"], r["dat"], r["att"],
    )
    wqkv, wp = r["wqkv"], r["wp"]
    tile_rows, tile_cols, width = scene.shape
    groups = width // GROUP
    pairs = tile_cols // 16
    row, col = lax.axis_index("row"), lax.axis_index("col")
    nrow, ncol = lax.axis_size("row"), lax.axis_size("col")
    x_at, z_at = row // 2, row % 2
    myself = row * ncol + col

    def at(drow, dcol):
        return {"row": (row + drow + nrow) % nrow, "col": (col + dcol + ncol) % ncol}

    def send(number, src, dst, device):
        return pltpu.make_async_remote_copy(
            src_ref=src,
            dst_ref=dst,
            send_sem=r["send_sems"].at[number],
            recv_sem=r["recv_sems"].at[number],
            device_id=device,
            device_id_type=pl.DeviceIdType.MESH,
        )

    barrier = pltpu.get_barrier_semaphore()
    partners = [(-1, 0), (1, 0), (0, -1), (0, 1), (2, 0), (-2, 0)]
    for partner in partners:
        pl.semaphore_signal(
            barrier, inc=1, device_id=at(*partner), device_id_type=pl.DeviceIdType.MESH
        )

    own = pl.ds(0, tile_rows)
    loads = [
        pltpu.make_async_copy(src, dst, r["load_sems"].at[k])
        for k, (src, dst) in enumerate(
            [
                (scene, xg.at[0, own, pl.ds(0, tile_cols)]),
                (cot, xg.at[1, own, pl.ds(0, tile_cols)]),
                (r["wqkv_hbm"], wqkv),
                (r["wp_hbm"], wp),
            ]
        )
    ]
    for load in loads:
        load.start()

    def row_halo(array, m):
        src = (scene, cot)[array]
        columns = pl.ds(m * 16, 16)
        return send(
            2 * m + array,
            src.at[pl.ds(0, HALF), columns],
            xg.at[array, pl.ds(tile_rows, HALF), columns],
            at(-1, 0),
        )

    low = lax.broadcasted_iota(jnp.int32, (WIN, width), 0) < HALF

    loads[0].wait()
    loads[1].wait()

    def pack_columns(k, _):
        for array in (0, 1):
            pair = xg[array, pl.ds(2 * k, 2), pl.ds(0, 16)].astype(F32)[:, :WIN]
            tile = jnp.where(low, pair[0], swap_halves(pair[1]))
            r["edge_f"][array, pl.ds(pl.multiple_of(k * WIN, WIN), WIN)] = tile
        return 0

    lax.fori_loop(0, tile_rows // 2, pack_columns, 0)
    r["edge_out"][...] = r["edge_f"][...].astype(BF16)

    edge_in, corner_in = r["edge_in"], r["corner_in"]
    tokens = tile_rows * HALF
    col_halo = send(8, r["edge_out"], edge_in, at(0, -1))
    corner = send(9, edge_in.at[:, pl.ds(0, 16)], corner_in, at(-1, 0))
    pl.semaphore_wait(barrier, len(partners))
    for m in (3, 2):
        for array in (0, 1):
            row_halo(array, m).start()
    col_halo.start()

    def unpack_columns(source, start, first_row, count):
        def body(k, _):
            for array in (0, 1):
                both = source[array, pl.ds(pl.multiple_of(start + k * 16, 16), 16)].astype(F32)
                for n in (0, 1):
                    tile = both[n * WIN : (n + 1) * WIN]
                    for odd in (0, 1):
                        part = swap_halves(tile) if odd else tile
                        whole = jnp.concatenate([part, jnp.zeros_like(part)], axis=0)
                        xg[array, first_row + 4 * k + 2 * n + odd, pl.ds(tile_cols, 16)] = (
                            whole.astype(BF16)
                        )
            return 0

        lax.fori_loop(0, count, body, 0)

    for load in loads[2:]:
        load.wait()
    wqkv_t, wp_t = r["wqkv_t"], r["wp_t"]
    for n in range(3):
        wqkv_t[n * width : (n + 1) * width] = wqkv[:, n * width : (n + 1) * width].T
    wp_t[...] = wp[...].T

    edge_ret, left_in, corner_mid = r["edge_ret"], r["left_in"], r["corner_mid"]
    col_back = send(
        10, edge_ret.at[pl.ds(0, tokens - 16)], left_in.at[pl.ds(16, tokens - 16)], at(0, 1)
    )
    corner_down = send(11, edge_ret.at[pl.ds(tokens - 16, 16)], corner_mid, at(1, 0))
    corner_right = send(12, corner_mid, left_in.at[pl.ds(0, 16)], at(0, 1))
    row_back = send(
        13, br.at[pl.ds(tile_rows, HALF)], br.at[pl.ds(0, HALF)], at(1, 0)
    )

    scale = HD ** (-0.5)
    lane_head = lax.broadcasted_iota(jnp.int32, (AREA, GROUP), 1) // HD
    key_at = lax.broadcasted_iota(jnp.int32, (AREA, PACK * AREA), 0)
    query_at = lax.broadcasted_iota(jnp.int32, (AREA, PACK * AREA), 1) % AREA
    row_differs = jnp.where(key_at // 32 != query_at // 32, 1, 0)
    col_differs = jnp.where((key_at % 8) // 4 != (query_at % 8) // 4, 1, 0)

    def spread(block):
        zero = jnp.zeros_like(block)
        return jnp.concatenate([jnp.where(lane_head == h, block, zero) for h in range(PACK)], axis=0)

    def gather_heads(full):
        total = full[:AREA]
        for h in range(1, PACK):
            total = jnp.where(lane_head == h, full[h * AREA : (h + 1) * AREA], total)
        return total

    grads = r["grads"]
    early = 6 * BATCH

    def gather_early(x, _):
        here = pl.ds(pl.multiple_of(x * (width // 4), 16), width // 4)
        for q in range(4):
            lhs = (stash_at if q == 3 else stash_xt)[here, :early]
            rhs = stash_g[:early] if q == 3 else stash_d[:early, q * width : (q + 1) * width]
            grads[q, here] = dot(lhs, rhs)
        return 0

    def step(p, _):
        i = p // pairs
        m = p + i * (2 * pairs - 1 - 2 * p)

        @pl.when(p == 2)
        def _():
            col_halo.wait_recv()
            corner.start()
            unpack_columns(edge_in, 16, HALF, (tile_rows - HALF) // 4)

        @pl.when(p == 4)
        def _():
            for array in (0, 1):
                row_halo(array, 3).wait_send()
            for array in (0, 1):
                row_halo(array, 1).start()
            for array in (0, 1):
                row_halo(array, 3).wait_recv()
            corner.wait_recv()
            unpack_columns(corner_in, 0, tile_rows, 1)

        @pl.when(p == 5)
        def _():
            col_back.start()
            for array in (0, 1):
                row_halo(array, 2).wait_send()
            for array in (0, 1):
                row_halo(array, 0).start()
            for array in (0, 1):
                row_halo(array, 2).wait_recv()

        @pl.when(p == 6)
        def _():
            lax.fori_loop(0, 4, gather_early, 0)
            for array in (0, 1):
                row_halo(array, 1).wait_recv()

        @pl.when(p == 7)
        def _():
            for array in (0, 1):
                row_halo(array, 0).wait_recv()

        first = pl.multiple_of(p * BATCH, BATCH)
        here = pl.ds(pl.multiple_of(16 * m, 16), 16)
        following = pl.ds(pl.multiple_of(16 * m + 16, 16), 16)
        keep = [r["kept"][WIN * i + 2 * m + w, myself].astype(F32) for w in range(2)]
        for rows in range(4):
            top = pl.ds(WIN * i + HALF + 2 * rows, 2)
            for array in (0, 1):
                t0 = xg[array, top, here].astype(F32)
                t1 = xg[array, top, following].astype(F32)
                lo, hi, nx = t0[:, :WIN], t0[:, WIN:], t1[:, :WIN]
                for w, (a, c) in enumerate(((lo, hi), (hi, nx))):
                    tile = jnp.where(low, c, a).reshape(2 * WIN, width)
                    start = w * AREA + 16 * rows
                    if array == 0:
                        mean = jnp.mean(tile, axis=-1, keepdims=True)
                        centred = tile - mean
                        inverse = lax.rsqrt(
                            jnp.mean(centred * centred, axis=-1, keepdims=True) + 1e-05
                        )
                        normed = centred * inverse
                        xh_s[start : start + 16] = normed
                        xb_s[start : start + 16] = normed.astype(BF16)
                        inv_s[start : start + 16] = jnp.broadcast_to(inverse, (16, 128))
                    else:
                        stash_g[pl.ds(pl.multiple_of(first + start, 16), 16)] = (
                            tile * keep[w]
                        ).astype(BF16)

        xb = xb_s[...]
        stash_xt[:, pl.ds(first, BATCH)] = xb.T
        for n in range(3):
            qkv_s[:, n * width : (n + 1) * width] = dot(
                xb, wqkv[:, n * width : (n + 1) * width]
            ).astype(BF16)
        dat_s[...] = dot(stash_g[pl.ds(first, BATCH)], wp_t[...]).astype(BF16)

        last_row = jnp.where(row == nrow - 1, i, 0)
        last_col = jnp.where(col == ncol - 1, m // (pairs - 1), 0)
        biases = [
            jnp.where(row_differs * last_row + col_differs * lc > 0, -100.0, 0.0)
            for lc in (0, last_col)
        ]

        def part(n, g):
            return slice(n * width + g * GROUP, n * width + (g + 1) * GROUP)

        units = [(w, g) for w in range(2) for g in range(groups)]
        near = [slice(w * AREA, (w + 1) * AREA) for w in range(2)]
        far = [pl.ds(pl.multiple_of(first + w * AREA, AREA), AREA) for w in range(2)]
        q, k, v = [[qkv_s[near[w], part(n, g)] for w, g in units] for n in range(3)]
        spread_q = [spread(block) for block in q]
        spread_d = [spread(dat_s[near[w], part(0, g)]) for w, g in units]
        scores = [
            dot(a, c, NT) * scale + biases[w] for (w, _), a, c in zip(units, k, spread_q)
        ]
        d_p = [dot(a, c, NT) for a, c in zip(v, spread_d)]
        expo = [jnp.exp(a - jnp.max(a, axis=0, keepdims=True)) for a in scores]
        probs = [a * (1.0 / jnp.sum(a, axis=0, keepdims=True)) for a in expo]
        pb = [a.astype(BF16) for a in probs]
        d_s = [
            (a * (c - jnp.sum(a * c, axis=0, keepdims=True)) * scale).astype(BF16)
            for a, c in zip(probs, d_p)
        ]
        attended = [dot(a, c, TN) for a, c in zip(pb, v)]
        d_v = [dot(a, c) for a, c in zip(pb, spread_d)]
        d_q = [dot(a, c, TN) for a, c in zip(d_s, k)]
        d_k = [dot(a, c) for a, c in zip(d_s, spread_q)]
        for n, (w, g) in enumerate(units):
            att_s[near[w], part(0, g)] = gather_heads(attended[n]).astype(BF16)
            stash_d[far[w], part(0, g)] = gather_heads(d_q[n]).astype(BF16)
            stash_d[far[w], part(1, g)] = d_k[n].astype(BF16)
            stash_d[far[w], part(2, g)] = d_v[n].astype(BF16)

        stash_at[:, pl.ds(first, BATCH)] = att_s[...].T
        r["dxh"][...] = dot(stash_d[pl.ds(first, BATCH)], wqkv_t[...])

        last = []
        for at_row in range(WIN):
            tiles = []
            for w in (0, 1):
                near_row = slice(w * AREA + WIN * at_row, w * AREA + WIN * (at_row + 1))
                grad, normed = r["dxh"][near_row], xh_s[near_row]
                inverse = inv_s[near_row][:, :1]
                tiles.append(
                    inverse
                    * (
                        grad
                        - jnp.mean(grad, axis=-1, keepdims=True)
                        - normed * jnp.mean(grad * normed, axis=-1, keepdims=True)
                    )
                )
            br[HALF + WIN * i + at_row, here] = jnp.concatenate(tiles, axis=0).astype(BF16)
            r["last"][at_row] = tiles[1]

        @pl.when(m == pairs - 1)
        def _():
            last = r["last"][...]
            packed = [
                jnp.where(low, last[2 * n], swap_halves(last[2 * n + 1])) for n in range(WIN // 2)
            ]
            edge_ret[pl.ds(pl.multiple_of(32 * i, 32), 32)] = jnp.concatenate(
                packed, axis=0
            ).astype(BF16)

        return 0

    lax.fori_loop(0, 2 * pairs, step, 0)
    corner_down.start()
    row_back.start()

    share = width // (nrow * ncol)
    parts = [r["part_%d" % q] for q in range(4)]

    def close_grads(q):
        def body(x, _):
            here = pl.ds(pl.multiple_of(x * (width // 4), 16), width // 4)
            lhs = (stash_at if q == 3 else stash_xt)[here, early:]
            rhs = stash_g[early:] if q == 3 else stash_d[early:, q * width : (q + 1) * width]
            block = grads[q, here] + dot(lhs, rhs)
            for z in range(2):
                for y in range(4):
                    piece = block[(4 * z + y) * share : (4 * z + y + 1) * share]
                    piece = jnp.concatenate(
                        [piece[:, : width // 2], piece[:, width // 2 :]], axis=0
                    ).astype(BF16)
                    if q < 2:
                        parts[q][x, z, y] = piece
                    else:
                        parts[q][y, z, x] = piece
            return 0

        lax.fori_loop(0, 4, body, 0, unroll=4)

    class Ring:
        def __init__(self, base, part, me, forward, backward, relay, direct):
            self.part, self.me, self.relay, self.direct = part, me, relay, direct
            ahead, behind, across = (me + 1) % 4, (me + 3) % 4, (me + 2) % 4
            self.ahead, self.behind = ahead, behind
            self.relay_back = send(base, part.at[across, 0], relay.at[0], backward)
            self.relay_on = send(base + 1, part.at[across, 1], relay.at[1], forward)
            self.own_on = send(base + 2, part.at[ahead, 0], direct.at[0, 0], forward)
            self.own_back = send(base + 3, part.at[behind, 1], direct.at[1, 1], backward)
            self.sum_back = send(base + 4, part.at[behind, 0], direct.at[1, 0], backward)
            self.sum_on = send(base + 5, part.at[ahead, 1], direct.at[0, 1], forward)

        def begin(self):
            self.relay_back.start()
            self.relay_on.start()

        def go_on(self):
            self.own_on.start()
            self.own_back.start()

        def pass_on(self):
            for n, copy, relayed, target in (
                (0, self.sum_back, self.relay_back, self.behind),
                (1, self.sum_on, self.relay_on, self.ahead),
            ):
                relayed.wait_recv()
                total = self.part[target, n].astype(F32) + self.relay[n].astype(F32)
                self.part[target, n] = total.astype(BF16)
                copy.start()

        def arrive(self):
            for copy in (self.own_on, self.own_back, self.sum_back, self.sum_on):
                copy.wait_recv()

        def total(self, z):
            return (
                self.part[self.me, z].astype(F32)
                + self.direct[0, z].astype(F32)
                + self.direct[1, z].astype(F32)
            )

        def close(self):
            for copy in (
                self.relay_back, self.relay_on, self.own_on,
                self.own_back, self.sum_back, self.sum_on,
            ):
                copy.wait_send()

    on_x = (x_at, at(2, 0), at(-2, 0))
    on_y = (col, at(0, 1), at(0, -1))
    outer, inner = [], []
    for q in range(4):
        axes = (on_x, on_y) if q < 2 else (on_y, on_x)
        for rings, name, axis, base in (
            (outer, "part_%d", axes[0], 16),
            (inner, "next_%d", axes[1], 40),
        ):
            rings.append(
                Ring(
                    base + 6 * q,
                    r[name % q],
                    *axis,
                    r["relay_" + name % q],
                    r["direct_" + name % q],
                )
            )

    def turn(q):
        outer[q].arrive()
        for z in range(2):
            total = outer[q].total(z).astype(BF16)
            for n in range(4):
                inner[q].part[n, z] = total[n]
        inner[q].begin()
        inner[q].go_on()

    last_out, last_in, mine = r["last_out"], r["last_in"], r["mine"]
    crossing = [send(64 + q, last_out.at[q], last_in.at[q], at(1 - 2 * z_at, 0)) for q in range(4)]

    def cross(q):
        inner[q].arrive()
        last_out[q] = inner[q].total(1 - z_at).astype(BF16)
        crossing[q].start()
        mine[q] = inner[q].total(z_at)

    def place(k, _):
        left = left_in[pl.ds(pl.multiple_of(16 * k, 16), 16)].astype(F32)
        for n in range(4):
            at_row = 4 * k + n
            tile = left[WIN * (n // 2) : WIN * (n // 2 + 1)]
            before = swap_halves(tile) if n % 2 else tile
            for m in range(pairs):
                here = slice(16 * m, 16 * m + 16)
                both = br[at_row, here].astype(F32)
                lo, hi = both[:WIN], both[WIN:]
                r["out"][at_row, here] = jnp.concatenate(
                    [jnp.where(low, before, lo), jnp.where(low, lo, hi)], axis=0
                ).astype(BF16)
                before = hi
        return 0

    order = (0, 2, 1, 3)
    for q in order:
        close_grads(q)
        outer[q].begin()
        outer[q].go_on()
    for q in order:
        outer[q].pass_on()
    col_back.wait_recv()
    lax.fori_loop(1, tile_rows // 4, place, 0)
    for q in order:
        turn(q)
    corner_down.wait_recv()
    corner_right.start()
    for q in order:
        inner[q].pass_on()
    row_back.wait_recv()
    corner_right.wait_recv()
    lax.fori_loop(0, 1, place, 0)
    for q in order:
        cross(q)
    for q in (0, 2, 1, 3):
        crossing[q].wait_recv()
        total = mine[q] + last_in[q].astype(F32)
        total = jnp.concatenate([total[:share], total[share:]], axis=1)
        if q < 3:
            r["qkv_grad"][:, q * width : (q + 1) * width] = total
        else:
            r["proj_grad"][...] = total

    for array in (0, 1):
        for m in (1, 0):
            row_halo(array, m).wait_send()
    for copy in (col_halo, corner, col_back, corner_down, corner_right, row_back, *crossing):
        copy.wait_send()
    for ring in (*outer, *inner):
        ring.close()


def on_device(scene, cotangent, query_key_value_weight, proj_weight, kept):
    rows, cols, width = scene.shape
    share = width // 32
    piece = (2 * share, width // 2)
    tokens = rows * HALF
    all_tokens = rows * cols
    vmem = {
        "xg": ((2, rows + HALF, cols + 16, width), BF16),
        "br": ((rows + HALF, cols, width), BF16),
        "stash_d": ((all_tokens, 3 * width), BF16),
        "stash_g": ((all_tokens, width), BF16),
        "stash_xt": ((width, all_tokens), BF16),
        "stash_at": ((width, all_tokens), BF16),
        "grads": ((4, width, width), F32),
        "xb": ((BATCH, width), BF16),
        "xh": ((BATCH, width), F32),
        "inv": ((BATCH, 128), F32),
        "qkv": ((BATCH, 3 * width), BF16),
        "dat": ((BATCH, width), BF16),
        "att": ((BATCH, width), BF16),
        "dxh": ((BATCH, width), F32),
        "last": ((WIN, WIN, width), F32),
        "wqkv": ((width, 3 * width), BF16),
        "wp": ((width, width), BF16),
        "wqkv_t": ((3 * width, width), BF16),
        "wp_t": ((width, width), BF16),
        "edge_f": ((2, tokens, width), F32),
        "edge_out": ((2, tokens, width), BF16),
        "edge_in": ((2, tokens, width), BF16),
        "corner_in": ((2, 16, width), BF16),
        "edge_ret": ((tokens, width), BF16),
        "left_in": ((tokens, width), BF16),
        "corner_mid": ((16, width), BF16),
        "last_out": ((4, *piece), BF16),
        "last_in": ((4, *piece), BF16),
        "mine": ((4, *piece), F32),
    }
    for q in range(4):
        vmem["part_%d" % q] = ((4, 2, 4, *piece), BF16)
        vmem["relay_part_%d" % q] = ((2, 4, *piece), BF16)
        vmem["direct_part_%d" % q] = ((2, 2, 4, *piece), BF16)
        vmem["next_%d" % q] = ((4, 2, *piece), BF16)
        vmem["relay_next_%d" % q] = ((2, *piece), BF16)
        vmem["direct_next_%d" % q] = ((2, 2, *piece), BF16)
    sems = {
        "load_sems": pltpu.SemaphoreType.DMA((4,)),
        "send_sems": pltpu.SemaphoreType.DMA((68,)),
        "recv_sems": pltpu.SemaphoreType.DMA((68,)),
    }
    names = (
        ["scene", "cotangent", "wqkv_hbm", "wp_hbm", "kept", "out", "qkv_grad", "proj_grad"]
        + list(vmem)
        + list(sems)
    )
    anywhere = pl.BlockSpec(memory_space=pl.ANY)
    in_vmem = pl.BlockSpec(memory_space=pltpu.VMEM)
    branch, qkv_grad, proj_grad = pl.pallas_call(
        functools.partial(kernel, names),
        out_shape=(
            jax.ShapeDtypeStruct((rows, cols, width), BF16),
            jax.ShapeDtypeStruct((share, 3 * width), F32),
            jax.ShapeDtypeStruct((share, width), F32),
        ),
        in_specs=[anywhere] * 4 + [pl.BlockSpec(memory_space=pltpu.SMEM)],
        out_specs=(in_vmem,) * 3,
        scratch_shapes=[pltpu.VMEM(*spec) for spec in vmem.values()] + list(sems.values()),
        compiler_params=pltpu.CompilerParams(
            collective_id=0, has_side_effects=True, vmem_limit_bytes=60 * 1024 * 1024
        ),
    )(scene, cotangent, query_key_value_weight, proj_weight, kept.T)
    scene_grad = (cotangent.astype(F32) + branch.astype(F32)).astype(BF16)
    return scene_grad, qkv_grad, proj_grad


def solution(mesh):
    return jax.shard_map(
        on_device,
        mesh=mesh,
        in_specs=(
            P(("scene", "row"), "col", None),
            P(("scene", "row"), "col", None),
            P(),
            P(),
            P("scene", None),
        ),
        out_specs=(
            P(("scene", "row"), "col", None),
            P(("scene", "row", "col"), None),
            P(("scene", "row", "col"), None),
        ),
        check_vma=False,
    )
```

```python
import functools

import jax
import jax.numpy as jnp
from jax import lax
from jax.experimental import pallas as pl
from jax.experimental.pallas import tpu as pltpu
from jax.sharding import PartitionSpec as P

HD = 32
WIN = 8
HALF = 4
AREA = 64
PACK = 4
GROUP = PACK * HD
BATCH = 2 * AREA
F32 = jnp.float32
BF16 = jnp.bfloat16
NT = (((1,), (1,)), ((), ()))
TN = (((0,), (0,)), ((), ()))


def dot(a, b, dims=(((1,), (0,)), ((), ()))):
    return lax.dot_general(a, b, dims, preferred_element_type=F32)


def swap_halves(tile):
    return pltpu.roll(tile, HALF, tile.ndim - 2)


def kernel(names, *refs):
    r = dict(zip(names, refs))
    scene, cot = r["scene"], r["cotangent"]
    xg, br, stash_d, stash_g = r["xg"], r["br"], r["stash_d"], r["stash_g"]
    stash_xt, stash_at = r["stash_xt"], r["stash_at"]
    xb_s, xh_s, inv_s, qkv_s, dat_s, att_s = (
        r["xb"], r["xh"], r["inv"], r["qkv"], r["dat"], r["att"],
    )
    wqkv, wp = r["wqkv"], r["wp"]
    tile_rows, tile_cols, width = scene.shape
    groups = width // GROUP
    pairs = tile_cols // 16
    row, col = lax.axis_index("row"), lax.axis_index("col")
    nrow, ncol = lax.axis_size("row"), lax.axis_size("col")
    x_at, z_at = row // 2, row % 2
    myself = row * ncol + col

    def at(drow, dcol):
        return {"row": (row + drow + nrow) % nrow, "col": (col + dcol + ncol) % ncol}

    def send(number, src, dst, device):
        return pltpu.make_async_remote_copy(
            src_ref=src,
            dst_ref=dst,
            send_sem=r["send_sems"].at[number],
            recv_sem=r["recv_sems"].at[number],
            device_id=device,
            device_id_type=pl.DeviceIdType.MESH,
        )

    barrier = pltpu.get_barrier_semaphore()
    partners = [(-1, 0), (1, 0), (0, -1), (0, 1), (2, 0), (-2, 0)]
    for partner in partners:
        pl.semaphore_signal(
            barrier, inc=1, device_id=at(*partner), device_id_type=pl.DeviceIdType.MESH
        )

    own = pl.ds(0, tile_rows)
    loads = [
        pltpu.make_async_copy(src, dst, r["load_sems"].at[k])
        for k, (src, dst) in enumerate(
            [
                (scene, xg.at[0, own, pl.ds(0, tile_cols)]),
                (cot, xg.at[1, own, pl.ds(0, tile_cols)]),
                (r["wqkv_hbm"], wqkv),
                (r["wp_hbm"], wp),
            ]
        )
    ]
    for load in loads:
        load.start()

    def row_halo(array, m):
        src = (scene, cot)[array]
        columns = pl.ds(m * 16, 16)
        return send(
            2 * m + array,
            src.at[pl.ds(0, HALF), columns],
            xg.at[array, pl.ds(tile_rows, HALF), columns],
            at(-1, 0),
        )

    low = lax.broadcasted_iota(jnp.int32, (WIN, width), 0) < HALF

    loads[0].wait()
    loads[1].wait()

    def pack_columns(k, _):
        for array in (0, 1):
            pair = xg[array, pl.ds(2 * k, 2), pl.ds(0, 16)].astype(F32)[:, :WIN]
            tile = jnp.where(low, pair[0], swap_halves(pair[1]))
            r["edge_f"][array, pl.ds(pl.multiple_of(k * WIN, WIN), WIN)] = tile
        return 0

    lax.fori_loop(0, tile_rows // 2, pack_columns, 0)
    r["edge_out"][...] = r["edge_f"][...].astype(BF16)

    edge_in, corner_in = r["edge_in"], r["corner_in"]
    tokens = tile_rows * HALF
    col_halo = send(8, r["edge_out"], edge_in, at(0, -1))
    corner = send(9, edge_in.at[:, pl.ds(0, 16)], corner_in, at(-1, 0))
    pl.semaphore_wait(barrier, len(partners))
    for m in (3, 2):
        for array in (0, 1):
            row_halo(array, m).start()
    col_halo.start()

    def unpack_columns(source, start, first_row, count):
        def body(k, _):
            for array in (0, 1):
                both = source[array, pl.ds(pl.multiple_of(start + k * 16, 16), 16)].astype(F32)
                for n in (0, 1):
                    tile = both[n * WIN : (n + 1) * WIN]
                    for odd in (0, 1):
                        part = swap_halves(tile) if odd else tile
                        whole = jnp.concatenate([part, jnp.zeros_like(part)], axis=0)
                        xg[array, first_row + 4 * k + 2 * n + odd, pl.ds(tile_cols, 16)] = (
                            whole.astype(BF16)
                        )
            return 0

        lax.fori_loop(0, count, body, 0)

    for load in loads[2:]:
        load.wait()
    wqkv_t, wp_t = r["wqkv_t"], r["wp_t"]
    for n in range(3):
        wqkv_t[n * width : (n + 1) * width] = wqkv[:, n * width : (n + 1) * width].T
    wp_t[...] = wp[...].T

    edge_ret, left_in, corner_mid = r["edge_ret"], r["left_in"], r["corner_mid"]
    col_back = send(
        10, edge_ret.at[pl.ds(0, tokens - 16)], left_in.at[pl.ds(16, tokens - 16)], at(0, 1)
    )
    corner_down = send(11, edge_ret.at[pl.ds(tokens - 16, 16)], corner_mid, at(1, 0))
    corner_right = send(12, corner_mid, left_in.at[pl.ds(0, 16)], at(0, 1))
    row_back = send(
        13, br.at[pl.ds(tile_rows, HALF)], br.at[pl.ds(0, HALF)], at(1, 0)
    )

    scale = HD ** (-0.5)
    lane_head = lax.broadcasted_iota(jnp.int32, (AREA, GROUP), 1) // HD
    key_at = lax.broadcasted_iota(jnp.int32, (AREA, PACK * AREA), 0)
    query_at = lax.broadcasted_iota(jnp.int32, (AREA, PACK * AREA), 1) % AREA
    row_differs = jnp.where(key_at // 32 != query_at // 32, 1, 0)
    col_differs = jnp.where((key_at % 8) // 4 != (query_at % 8) // 4, 1, 0)

    def spread(block):
        zero = jnp.zeros_like(block)
        return jnp.concatenate([jnp.where(lane_head == h, block, zero) for h in range(PACK)], axis=0)

    def gather_heads(full):
        total = full[:AREA]
        for h in range(1, PACK):
            total = jnp.where(lane_head == h, full[h * AREA : (h + 1) * AREA], total)
        return total

    grads = r["grads"]
    early = 6 * BATCH

    def gather_early(x, _):
        here = pl.ds(pl.multiple_of(x * (width // 4), 16), width // 4)
        for q in range(4):
            lhs = (stash_at if q == 3 else stash_xt)[here, :early]
            rhs = stash_g[:early] if q == 3 else stash_d[:early, q * width : (q + 1) * width]
            grads[q, here] = dot(lhs, rhs)
        return 0

    def step(p, _):
        i = p // pairs
        m = p + i * (2 * pairs - 1 - 2 * p)

        @pl.when(p == 2)
        def _():
            col_halo.wait_recv()
            corner.start()
            unpack_columns(edge_in, 16, HALF, (tile_rows - HALF) // 4)

        @pl.when(p == 4)
        def _():
            for array in (0, 1):
                row_halo(array, 3).wait_send()
            for array in (0, 1):
                row_halo(array, 1).start()
            for array in (0, 1):
                row_halo(array, 3).wait_recv()
            corner.wait_recv()
            unpack_columns(corner_in, 0, tile_rows, 1)

        @pl.when(p == 5)
        def _():
            col_back.start()
            for array in (0, 1):
                row_halo(array, 2).wait_send()
            for array in (0, 1):
                row_halo(array, 0).start()
            for array in (0, 1):
                row_halo(array, 2).wait_recv()

        @pl.when(p == 6)
        def _():
            lax.fori_loop(0, 4, gather_early, 0)
            for array in (0, 1):
                row_halo(array, 1).wait_recv()

        @pl.when(p == 7)
        def _():
            for array in (0, 1):
                row_halo(array, 0).wait_recv()

        first = pl.multiple_of(p * BATCH, BATCH)
        here = pl.ds(pl.multiple_of(16 * m, 16), 16)
        following = pl.ds(pl.multiple_of(16 * m + 16, 16), 16)
        keep = [r["kept"][WIN * i + 2 * m + w, myself].astype(F32) for w in range(2)]
        for rows in range(4):
            top = pl.ds(WIN * i + HALF + 2 * rows, 2)
            for array in (0, 1):
                t0 = xg[array, top, here].astype(F32)
                t1 = xg[array, top, following].astype(F32)
                lo, hi, nx = t0[:, :WIN], t0[:, WIN:], t1[:, :WIN]
                for w, (a, c) in enumerate(((lo, hi), (hi, nx))):
                    tile = jnp.where(low, c, a).reshape(2 * WIN, width)
                    start = w * AREA + 16 * rows
                    if array == 0:
                        mean = jnp.mean(tile, axis=-1, keepdims=True)
                        centred = tile - mean
                        inverse = lax.rsqrt(
                            jnp.mean(centred * centred, axis=-1, keepdims=True) + 1e-05
                        )
                        normed = centred * inverse
                        xh_s[start : start + 16] = normed
                        xb_s[start : start + 16] = normed.astype(BF16)
                        inv_s[start : start + 16] = jnp.broadcast_to(inverse, (16, 128))
                    else:
                        stash_g[pl.ds(pl.multiple_of(first + start, 16), 16)] = (
                            tile * keep[w]
                        ).astype(BF16)

        xb = xb_s[...]
        stash_xt[:, pl.ds(first, BATCH)] = xb.T
        for n in range(3):
            qkv_s[:, n * width : (n + 1) * width] = dot(
                xb, wqkv[:, n * width : (n + 1) * width]
            ).astype(BF16)
        dat_s[...] = dot(stash_g[pl.ds(first, BATCH)], wp_t[...]).astype(BF16)

        last_row = jnp.where(row == nrow - 1, i, 0)
        last_col = jnp.where(col == ncol - 1, m // (pairs - 1), 0)
        biases = [
            jnp.where(row_differs * last_row + col_differs * lc > 0, -100.0, 0.0)
            for lc in (0, last_col)
        ]

        def part(n, g):
            return slice(n * width + g * GROUP, n * width + (g + 1) * GROUP)

        units = [(w, g) for w in range(2) for g in range(groups)]
        near = [slice(w * AREA, (w + 1) * AREA) for w in range(2)]
        far = [pl.ds(pl.multiple_of(first + w * AREA, AREA), AREA) for w in range(2)]
        q, k, v = [[qkv_s[near[w], part(n, g)] for w, g in units] for n in range(3)]
        spread_q = [spread(block) for block in q]
        spread_d = [spread(dat_s[near[w], part(0, g)]) for w, g in units]
        scores = [
            dot(a, c, NT) * scale + biases[w] for (w, _), a, c in zip(units, k, spread_q)
        ]
        d_p = [dot(a, c, NT) for a, c in zip(v, spread_d)]
        expo = [jnp.exp(a - jnp.max(a, axis=0, keepdims=True)) for a in scores]
        probs = [a * (1.0 / jnp.sum(a, axis=0, keepdims=True)) for a in expo]
        pb = [a.astype(BF16) for a in probs]
        d_s = [
            (a * (c - jnp.sum(a * c, axis=0, keepdims=True)) * scale).astype(BF16)
            for a, c in zip(probs, d_p)
        ]
        attended = [dot(a, c, TN) for a, c in zip(pb, v)]
        d_v = [dot(a, c) for a, c in zip(pb, spread_d)]
        d_q = [dot(a, c, TN) for a, c in zip(d_s, k)]
        d_k = [dot(a, c) for a, c in zip(d_s, spread_q)]
        for n, (w, g) in enumerate(units):
            att_s[near[w], part(0, g)] = gather_heads(attended[n]).astype(BF16)
            stash_d[far[w], part(0, g)] = gather_heads(d_q[n]).astype(BF16)
            stash_d[far[w], part(1, g)] = d_k[n].astype(BF16)
            stash_d[far[w], part(2, g)] = d_v[n].astype(BF16)

        stash_at[:, pl.ds(first, BATCH)] = att_s[...].T
        r["dxh"][...] = dot(stash_d[pl.ds(first, BATCH)], wqkv_t[...])

        last = []
        for at_row in range(WIN):
            tiles = []
            for w in (0, 1):
                near_row = slice(w * AREA + WIN * at_row, w * AREA + WIN * (at_row + 1))
                grad, normed = r["dxh"][near_row], xh_s[near_row]
                inverse = inv_s[near_row][:, :1]
                tiles.append(
                    inverse
                    * (
                        grad
                        - jnp.mean(grad, axis=-1, keepdims=True)
                        - normed * jnp.mean(grad * normed, axis=-1, keepdims=True)
                    )
                )
            br[HALF + WIN * i + at_row, here] = jnp.concatenate(tiles, axis=0).astype(BF16)
            r["last"][at_row] = tiles[1]

        @pl.when(m == pairs - 1)
        def _():
            last = r["last"][...]
            packed = [
                jnp.where(low, last[2 * n], swap_halves(last[2 * n + 1])) for n in range(WIN // 2)
            ]
            edge_ret[pl.ds(pl.multiple_of(32 * i, 32), 32)] = jnp.concatenate(
                packed, axis=0
            ).astype(BF16)

        return 0

    lax.fori_loop(0, 2 * pairs, step, 0)
    corner_down.start()
    row_back.start()

    share = width // (nrow * ncol)
    parts = [r["part_%d" % q] for q in range(4)]

    def close_grads(q):
        def body(x, _):
            here = pl.ds(pl.multiple_of(x * (width // 4), 16), width // 4)
            lhs = (stash_at if q == 3 else stash_xt)[here, early:]
            rhs = stash_g[early:] if q == 3 else stash_d[early:, q * width : (q + 1) * width]
            block = grads[q, here] + dot(lhs, rhs)
            for z in range(2):
                for y in range(4):
                    piece = block[(4 * z + y) * share : (4 * z + y + 1) * share]
                    piece = jnp.concatenate(
                        [piece[:, : width // 2], piece[:, width // 2 :]], axis=0
                    ).astype(BF16)
                    if q < 2:
                        parts[q][x, z, y] = piece
                    else:
                        parts[q][y, z, x] = piece
            return 0

        lax.fori_loop(0, 4, body, 0, unroll=4)

    class Ring:
        def __init__(self, base, part, me, forward, backward, relay, direct):
            self.part, self.me, self.relay, self.direct = part, me, relay, direct
            ahead, behind, across = (me + 1) % 4, (me + 3) % 4, (me + 2) % 4
            self.ahead, self.behind = ahead, behind
            self.relay_back = send(base, part.at[across, 0], relay.at[0], backward)
            self.relay_on = send(base + 1, part.at[across, 1], relay.at[1], forward)
            self.own_on = send(base + 2, part.at[ahead, 0], direct.at[0, 0], forward)
            self.own_back = send(base + 3, part.at[behind, 1], direct.at[1, 1], backward)
            self.sum_back = send(base + 4, part.at[behind, 0], direct.at[1, 0], backward)
            self.sum_on = send(base + 5, part.at[ahead, 1], direct.at[0, 1], forward)

        def begin(self):
            self.relay_back.start()
            self.relay_on.start()

        def go_on(self):
            self.own_on.start()
            self.own_back.start()

        def pass_on(self):
            for n, copy, relayed, target in (
                (0, self.sum_back, self.relay_back, self.behind),
                (1, self.sum_on, self.relay_on, self.ahead),
            ):
                relayed.wait_recv()
                total = self.part[target, n].astype(F32) + self.relay[n].astype(F32)
                self.part[target, n] = total.astype(BF16)
                copy.start()

        def arrive(self):
            for copy in (self.own_on, self.own_back, self.sum_back, self.sum_on):
                copy.wait_recv()

        def total(self, z):
            return (
                self.part[self.me, z].astype(F32)
                + self.direct[0, z].astype(F32)
                + self.direct[1, z].astype(F32)
            )

        def close(self):
            for copy in (
                self.relay_back, self.relay_on, self.own_on,
                self.own_back, self.sum_back, self.sum_on,
            ):
                copy.wait_send()

    on_x = (x_at, at(2, 0), at(-2, 0))
    on_y = (col, at(0, 1), at(0, -1))
    outer, inner = [], []
    for q in range(4):
        axes = (on_x, on_y) if q < 2 else (on_y, on_x)
        for rings, name, axis, base in (
            (outer, "part_%d", axes[0], 16),
            (inner, "next_%d", axes[1], 40),
        ):
            rings.append(
                Ring(
                    base + 6 * q,
                    r[name % q],
                    *axis,
                    r["relay_" + name % q],
                    r["direct_" + name % q],
                )
            )

    def turn(q):
        outer[q].arrive()
        for z in range(2):
            total = outer[q].total(z).astype(BF16)
            for n in range(4):
                inner[q].part[n, z] = total[n]
        inner[q].begin()
        inner[q].go_on()

    last_out, last_in, mine = r["last_out"], r["last_in"], r["mine"]
    crossing = [send(64 + q, last_out.at[q], last_in.at[q], at(1 - 2 * z_at, 0)) for q in range(4)]

    def cross(q):
        inner[q].arrive()
        last_out[q] = inner[q].total(1 - z_at).astype(BF16)
        crossing[q].start()
        mine[q] = inner[q].total(z_at)

    def place(k, _):
        left = left_in[pl.ds(pl.multiple_of(16 * k, 16), 16)].astype(F32)
        for n in range(4):
            at_row = 4 * k + n
            tile = left[WIN * (n // 2) : WIN * (n // 2 + 1)]
            before = swap_halves(tile) if n % 2 else tile
            for m in range(pairs):
                here = slice(16 * m, 16 * m + 16)
                both = br[at_row, here].astype(F32)
                lo, hi = both[:WIN], both[WIN:]
                grad = jnp.concatenate(
                    [jnp.where(low, before, lo), jnp.where(low, lo, hi)], axis=0
                )
                r["out"][at_row, here] = (xg[1, at_row, here].astype(F32) + grad).astype(BF16)
                before = hi
        return 0

    order = (0, 2, 1, 3)
    for q in order:
        close_grads(q)
        outer[q].begin()
        outer[q].go_on()
    for q in order:
        outer[q].pass_on()
    col_back.wait_recv()
    lax.fori_loop(1, tile_rows // 4, place, 0)
    for q in order:
        turn(q)
    corner_down.wait_recv()
    corner_right.start()
    for q in order:
        inner[q].pass_on()
    row_back.wait_recv()
    corner_right.wait_recv()
    lax.fori_loop(0, 1, place, 0)
    for q in order:
        cross(q)
    for q in (0, 2, 1, 3):
        crossing[q].wait_recv()
        total = mine[q] + last_in[q].astype(F32)
        total = jnp.concatenate([total[:share], total[share:]], axis=1)
        if q < 3:
            r["qkv_grad"][:, q * width : (q + 1) * width] = total
        else:
            r["proj_grad"][...] = total

    for array in (0, 1):
        for m in (1, 0):
            row_halo(array, m).wait_send()
    for copy in (col_halo, corner, col_back, corner_down, corner_right, row_back, *crossing):
        copy.wait_send()
    for ring in (*outer, *inner):
        ring.close()


def hand_over(scene_in, qkv_in, proj_in, scene_grad, qkv_grad, proj_grad, a, b, c, come, go):
    step = scene_in.shape[0] // 8
    pieces = [(qkv_in, b, qkv_grad), (proj_in, c, proj_grad)]
    for n in range(8):
        here = pl.ds(n * step, step)
        pieces.append((scene_in.at[here], a.at[here], scene_grad.at[here]))
    loads = [pltpu.make_async_copy(x, y, come.at[n]) for n, (x, y, _) in enumerate(pieces)]
    stores = [pltpu.make_async_copy(y, z, go.at[n]) for n, (_, y, z) in enumerate(pieces)]
    for load in loads:
        load.start()
    for load, store in zip(loads, stores):
        load.wait()
        store.start()
    for store in stores:
        store.wait()


def on_device(scene, cotangent, query_key_value_weight, proj_weight, kept):
    rows, cols, width = scene.shape
    share = width // 32
    piece = (2 * share, width // 2)
    tokens = rows * HALF
    all_tokens = rows * cols
    vmem = {
        "xg": ((2, rows + HALF, cols + 16, width), BF16),
        "br": ((rows + HALF, cols, width), BF16),
        "stash_d": ((all_tokens, 3 * width), BF16),
        "stash_g": ((all_tokens, width), BF16),
        "stash_xt": ((width, all_tokens), BF16),
        "stash_at": ((width, all_tokens), BF16),
        "grads": ((4, width, width), F32),
        "xb": ((BATCH, width), BF16),
        "xh": ((BATCH, width), F32),
        "inv": ((BATCH, 128), F32),
        "qkv": ((BATCH, 3 * width), BF16),
        "dat": ((BATCH, width), BF16),
        "att": ((BATCH, width), BF16),
        "dxh": ((BATCH, width), F32),
        "last": ((WIN, WIN, width), F32),
        "wqkv": ((width, 3 * width), BF16),
        "wp": ((width, width), BF16),
        "wqkv_t": ((3 * width, width), BF16),
        "wp_t": ((width, width), BF16),
        "edge_f": ((2, tokens, width), F32),
        "edge_out": ((2, tokens, width), BF16),
        "edge_in": ((2, tokens, width), BF16),
        "corner_in": ((2, 16, width), BF16),
        "edge_ret": ((tokens, width), BF16),
        "left_in": ((tokens, width), BF16),
        "corner_mid": ((16, width), BF16),
        "last_out": ((4, *piece), BF16),
        "last_in": ((4, *piece), BF16),
        "mine": ((4, *piece), F32),
    }
    for q in range(4):
        vmem["part_%d" % q] = ((4, 2, 4, *piece), BF16)
        vmem["relay_part_%d" % q] = ((2, 4, *piece), BF16)
        vmem["direct_part_%d" % q] = ((2, 2, 4, *piece), BF16)
        vmem["next_%d" % q] = ((4, 2, *piece), BF16)
        vmem["relay_next_%d" % q] = ((2, *piece), BF16)
        vmem["direct_next_%d" % q] = ((2, 2, *piece), BF16)
    sems = {
        "load_sems": pltpu.SemaphoreType.DMA((4,)),
        "send_sems": pltpu.SemaphoreType.DMA((68,)),
        "recv_sems": pltpu.SemaphoreType.DMA((68,)),
    }
    names = (
        ["scene", "cotangent", "wqkv_hbm", "wp_hbm", "kept", "out", "qkv_grad", "proj_grad"]
        + list(vmem)
        + list(sems)
    )
    anywhere = pl.BlockSpec(memory_space=pl.ANY)
    in_vmem = pl.BlockSpec(memory_space=pltpu.VMEM)
    grads = pl.pallas_call(
        functools.partial(kernel, names),
        out_shape=(
            jax.ShapeDtypeStruct((rows, cols, width), BF16),
            jax.ShapeDtypeStruct((share, 3 * width), F32),
            jax.ShapeDtypeStruct((share, width), F32),
        ),
        in_specs=[anywhere] * 4 + [pl.BlockSpec(memory_space=pltpu.SMEM)],
        out_specs=(in_vmem,) * 3,
        scratch_shapes=[pltpu.VMEM(*spec) for spec in vmem.values()] + list(sems.values()),
        compiler_params=pltpu.CompilerParams(
            collective_id=0, has_side_effects=True, vmem_limit_bytes=60 * 1024 * 1024
        ),
    )(scene, cotangent, query_key_value_weight, proj_weight, kept.T)
    return pl.pallas_call(
        hand_over,
        out_shape=tuple(jax.ShapeDtypeStruct(a.shape, a.dtype) for a in grads),
        in_specs=[anywhere] * 3,
        out_specs=(anywhere,) * 3,
        scratch_shapes=[pltpu.VMEM(a.shape, a.dtype) for a in grads]
        + [pltpu.SemaphoreType.DMA((10,)), pltpu.SemaphoreType.DMA((10,))],
    )(*grads)


def solution(mesh):
    return jax.shard_map(
        on_device,
        mesh=mesh,
        in_specs=(
            P(("scene", "row"), "col", None),
            P(("scene", "row"), "col", None),
            P(),
            P(),
            P("scene", None),
        ),
        out_specs=(
            P(("scene", "row"), "col", None),
            P(("scene", "row", "col"), None),
            P(("scene", "row", "col"), None),
        ),
        check_vma=False,
    )
```

```python
import functools

import jax
import jax.numpy as jnp
from jax import lax
from jax.experimental import pallas as pl
from jax.experimental.pallas import tpu as pltpu
from jax.sharding import PartitionSpec as P

HD = 32
WIN = 8
HALF = 4
AREA = 64
PACK = 4
GROUP = PACK * HD
BATCH = 2 * AREA
F32 = jnp.float32
BF16 = jnp.bfloat16
NT = (((1,), (1,)), ((), ()))
TN = (((0,), (0,)), ((), ()))


def dot(a, b, dims=(((1,), (0,)), ((), ()))):
    return lax.dot_general(a, b, dims, preferred_element_type=F32)


def swap_halves(tile):
    return pltpu.roll(tile, HALF, tile.ndim - 2)


def kernel(names, *refs):
    r = dict(zip(names, refs))
    scene, cot = r["scene"], r["cotangent"]
    xg, br, stash_d, stash_g = r["xg"], r["br"], r["stash_d"], r["stash_g"]
    stash_xt, stash_at = r["stash_xt"], r["stash_at"]
    xb_s, xh_s, inv_s, qkv_s, dat_s, att_s = (
        r["xb"], r["xh"], r["inv"], r["qkv"], r["dat"], r["att"],
    )
    wqkv, wp = r["wqkv"], r["wp"]
    tile_rows, tile_cols, width = scene.shape
    groups = width // GROUP
    pairs = tile_cols // 16
    row, col = lax.axis_index("row"), lax.axis_index("col")
    nrow, ncol = lax.axis_size("row"), lax.axis_size("col")
    x_at, z_at = row // 2, row % 2
    myself = row * ncol + col

    def at(drow, dcol):
        return {"row": (row + drow + nrow) % nrow, "col": (col + dcol + ncol) % ncol}

    def send(number, src, dst, device):
        return pltpu.make_async_remote_copy(
            src_ref=src,
            dst_ref=dst,
            send_sem=r["send_sems"].at[number],
            recv_sem=r["recv_sems"].at[number],
            device_id=device,
            device_id_type=pl.DeviceIdType.MESH,
        )

    barrier = pltpu.get_barrier_semaphore()
    partners = [(-1, 0), (1, 0), (0, -1), (0, 1), (2, 0), (-2, 0)]
    for partner in partners:
        pl.semaphore_signal(
            barrier, inc=1, device_id=at(*partner), device_id_type=pl.DeviceIdType.MESH
        )

    own = pl.ds(0, tile_rows)
    loads = [
        pltpu.make_async_copy(src, dst, r["load_sems"].at[k])
        for k, (src, dst) in enumerate(
            [
                (scene, xg.at[0, own, pl.ds(0, tile_cols)]),
                (cot, xg.at[1, own, pl.ds(0, tile_cols)]),
                (r["wqkv_hbm"], wqkv),
                (r["wp_hbm"], wp),
            ]
        )
    ]
    for load in loads:
        load.start()

    def row_halo(array, m):
        src = (scene, cot)[array]
        columns = pl.ds(m * 16, 16)
        return send(
            2 * m + array,
            src.at[pl.ds(0, HALF), columns],
            xg.at[array, pl.ds(tile_rows, HALF), columns],
            at(-1, 0),
        )

    low = lax.broadcasted_iota(jnp.int32, (WIN, width), 0) < HALF

    loads[0].wait()
    loads[1].wait()

    def pack_columns(k, _):
        for array in (0, 1):
            pair = xg[array, pl.ds(2 * k, 2), pl.ds(0, 16)].astype(F32)[:, :WIN]
            tile = jnp.where(low, pair[0], swap_halves(pair[1]))
            r["edge_f"][array, pl.ds(pl.multiple_of(k * WIN, WIN), WIN)] = tile
        return 0

    lax.fori_loop(0, tile_rows // 2, pack_columns, 0)
    r["edge_out"][...] = r["edge_f"][...].astype(BF16)

    edge_in, corner_in = r["edge_in"], r["corner_in"]
    tokens = tile_rows * HALF
    col_halo = send(8, r["edge_out"], edge_in, at(0, -1))
    corner = send(9, edge_in.at[:, pl.ds(0, 16)], corner_in, at(-1, 0))
    pl.semaphore_wait(barrier, len(partners))
    for m in (3, 2):
        for array in (0, 1):
            row_halo(array, m).start()
    col_halo.start()

    def unpack_columns(source, start, first_row, count):
        def body(k, _):
            for array in (0, 1):
                both = source[array, pl.ds(pl.multiple_of(start + k * 16, 16), 16)].astype(F32)
                for n in (0, 1):
                    tile = both[n * WIN : (n + 1) * WIN]
                    for odd in (0, 1):
                        part = swap_halves(tile) if odd else tile
                        whole = jnp.concatenate([part, jnp.zeros_like(part)], axis=0)
                        xg[array, first_row + 4 * k + 2 * n + odd, pl.ds(tile_cols, 16)] = (
                            whole.astype(BF16)
                        )
            return 0

        lax.fori_loop(0, count, body, 0)

    for load in loads[2:]:
        load.wait()
    wqkv_t, wp_t = r["wqkv_t"], r["wp_t"]
    for n in range(3):
        wqkv_t[n * width : (n + 1) * width] = wqkv[:, n * width : (n + 1) * width].T
    wp_t[...] = wp[...].T

    edge_ret, left_in, corner_mid = r["edge_ret"], r["left_in"], r["corner_mid"]
    col_back = send(
        10, edge_ret.at[pl.ds(0, tokens - 16)], left_in.at[pl.ds(16, tokens - 16)], at(0, 1)
    )
    corner_down = send(11, edge_ret.at[pl.ds(tokens - 16, 16)], corner_mid, at(1, 0))
    corner_right = send(12, corner_mid, left_in.at[pl.ds(0, 16)], at(0, 1))
    row_back = send(
        13, br.at[pl.ds(tile_rows, HALF)], br.at[pl.ds(0, HALF)], at(1, 0)
    )

    scale = HD ** (-0.5)
    lane_head = lax.broadcasted_iota(jnp.int32, (AREA, GROUP), 1) // HD
    key_at = lax.broadcasted_iota(jnp.int32, (AREA, PACK * AREA), 0)
    query_at = lax.broadcasted_iota(jnp.int32, (AREA, PACK * AREA), 1) % AREA
    row_differs = jnp.where(key_at // 32 != query_at // 32, 1, 0)
    col_differs = jnp.where((key_at % 8) // 4 != (query_at % 8) // 4, 1, 0)

    def spread(block):
        zero = jnp.zeros_like(block)
        return jnp.concatenate([jnp.where(lane_head == h, block, zero) for h in range(PACK)], axis=0)

    def gather_heads(full):
        total = full[:AREA]
        for h in range(1, PACK):
            total = jnp.where(lane_head == h, full[h * AREA : (h + 1) * AREA], total)
        return total

    grads = r["grads"]
    early = 6 * BATCH

    def gather_early(x, _):
        here = pl.ds(pl.multiple_of(x * (width // 4), 16), width // 4)
        for q in range(4):
            lhs = (stash_at if q == 3 else stash_xt)[here, :early]
            rhs = stash_g[:early] if q == 3 else stash_d[:early, q * width : (q + 1) * width]
            grads[q, here] = dot(lhs, rhs)
        return 0

    def place_of(p):
        i = p // pairs
        return i, p + i * (2 * pairs - 1 - 2 * p)

    def finish(p):
        i, m = place_of(p)
        first = pl.multiple_of(p * BATCH, BATCH)
        here = pl.ds(pl.multiple_of(16 * m, 16), 16)
        r["dxh"][...] = dot(stash_d[pl.ds(first, BATCH)], wqkv_t[...])

        last = []
        for at_row in range(WIN):
            tiles = []
            for w in (0, 1):
                near_row = slice(w * AREA + WIN * at_row, w * AREA + WIN * (at_row + 1))
                grad, normed = r["dxh"][near_row], xh_s[near_row]
                inverse = inv_s[near_row][:, :1]
                tiles.append(
                    inverse
                    * (
                        grad
                        - jnp.mean(grad, axis=-1, keepdims=True)
                        - normed * jnp.mean(grad * normed, axis=-1, keepdims=True)
                    )
                )
            br[HALF + WIN * i + at_row, here] = jnp.concatenate(tiles, axis=0).astype(BF16)
            r["last"][at_row] = tiles[1]

        @pl.when(m == pairs - 1)
        def _():
            last = r["last"][...]
            packed = [
                jnp.where(low, last[2 * n], swap_halves(last[2 * n + 1])) for n in range(WIN // 2)
            ]
            edge_ret[pl.ds(pl.multiple_of(32 * i, 32), 32)] = jnp.concatenate(
                packed, axis=0
            ).astype(BF16)

    def step(p, _):
        i, m = place_of(p)

        @pl.when(p > 0)
        def _():
            finish(p - 1)

        @pl.when(p == 2)
        def _():
            col_halo.wait_recv()
            corner.start()
            unpack_columns(edge_in, 16, HALF, (tile_rows - HALF) // 4)

        @pl.when(p == 4)
        def _():
            for array in (0, 1):
                row_halo(array, 3).wait_send()
            for array in (0, 1):
                row_halo(array, 1).start()
            for array in (0, 1):
                row_halo(array, 3).wait_recv()
            corner.wait_recv()
            unpack_columns(corner_in, 0, tile_rows, 1)

        @pl.when(p == 5)
        def _():
            col_back.start()
            for array in (0, 1):
                row_halo(array, 2).wait_send()
            for array in (0, 1):
                row_halo(array, 0).start()
            for array in (0, 1):
                row_halo(array, 2).wait_recv()

        @pl.when(p == 6)
        def _():
            lax.fori_loop(0, 4, gather_early, 0)
            for array in (0, 1):
                row_halo(array, 1).wait_recv()

        @pl.when(p == 7)
        def _():
            for array in (0, 1):
                row_halo(array, 0).wait_recv()

        first = pl.multiple_of(p * BATCH, BATCH)
        here = pl.ds(pl.multiple_of(16 * m, 16), 16)
        following = pl.ds(pl.multiple_of(16 * m + 16, 16), 16)
        keep = [r["kept"][WIN * i + 2 * m + w, myself].astype(F32) for w in range(2)]
        for rows in range(4):
            top = pl.ds(WIN * i + HALF + 2 * rows, 2)
            for array in (0, 1):
                t0 = xg[array, top, here].astype(F32)
                t1 = xg[array, top, following].astype(F32)
                lo, hi, nx = t0[:, :WIN], t0[:, WIN:], t1[:, :WIN]
                for w, (a, c) in enumerate(((lo, hi), (hi, nx))):
                    tile = jnp.where(low, c, a).reshape(2 * WIN, width)
                    start = w * AREA + 16 * rows
                    if array == 0:
                        mean = jnp.mean(tile, axis=-1, keepdims=True)
                        centred = tile - mean
                        inverse = lax.rsqrt(
                            jnp.mean(centred * centred, axis=-1, keepdims=True) + 1e-05
                        )
                        normed = centred * inverse
                        xh_s[start : start + 16] = normed
                        xb_s[start : start + 16] = normed.astype(BF16)
                        inv_s[start : start + 16] = jnp.broadcast_to(inverse, (16, 128))
                    else:
                        stash_g[pl.ds(pl.multiple_of(first + start, 16), 16)] = (
                            tile * keep[w]
                        ).astype(BF16)

        xb = xb_s[...]
        stash_xt[:, pl.ds(first, BATCH)] = xb.T
        for n in range(3):
            qkv_s[:, n * width : (n + 1) * width] = dot(
                xb, wqkv[:, n * width : (n + 1) * width]
            ).astype(BF16)
        dat_s[...] = dot(stash_g[pl.ds(first, BATCH)], wp_t[...]).astype(BF16)

        last_row = jnp.where(row == nrow - 1, i, 0)
        last_col = jnp.where(col == ncol - 1, m // (pairs - 1), 0)
        biases = [
            jnp.where(row_differs * last_row + col_differs * lc > 0, -100.0, 0.0)
            for lc in (0, last_col)
        ]

        def part(n, g):
            return slice(n * width + g * GROUP, n * width + (g + 1) * GROUP)

        units = [(w, g) for w in range(2) for g in range(groups)]
        near = [slice(w * AREA, (w + 1) * AREA) for w in range(2)]
        far = [pl.ds(pl.multiple_of(first + w * AREA, AREA), AREA) for w in range(2)]
        q, k, v = [[qkv_s[near[w], part(n, g)] for w, g in units] for n in range(3)]
        spread_q = [spread(block) for block in q]
        spread_d = [spread(dat_s[near[w], part(0, g)]) for w, g in units]
        scores = [
            dot(a, c, NT) * scale + biases[w] for (w, _), a, c in zip(units, k, spread_q)
        ]
        d_p = [dot(a, c, NT) for a, c in zip(v, spread_d)]
        expo = [jnp.exp(a - jnp.max(a, axis=0, keepdims=True)) for a in scores]
        probs = [a * (1.0 / jnp.sum(a, axis=0, keepdims=True)) for a in expo]
        pb = [a.astype(BF16) for a in probs]
        d_s = [
            (a * (c - jnp.sum(a * c, axis=0, keepdims=True)) * scale).astype(BF16)
            for a, c in zip(probs, d_p)
        ]
        attended = [dot(a, c, TN) for a, c in zip(pb, v)]
        d_v = [dot(a, c) for a, c in zip(pb, spread_d)]
        d_q = [dot(a, c, TN) for a, c in zip(d_s, k)]
        d_k = [dot(a, c) for a, c in zip(d_s, spread_q)]
        for n, (w, g) in enumerate(units):
            att_s[near[w], part(0, g)] = gather_heads(attended[n]).astype(BF16)
            stash_d[far[w], part(0, g)] = gather_heads(d_q[n]).astype(BF16)
            stash_d[far[w], part(1, g)] = d_k[n].astype(BF16)
            stash_d[far[w], part(2, g)] = d_v[n].astype(BF16)

        stash_at[:, pl.ds(first, BATCH)] = att_s[...].T
        return 0

    lax.fori_loop(0, 2 * pairs, step, 0)

    share = width // (nrow * ncol)
    parts = [r["part_%d" % q] for q in range(4)]

    def close_grads(q):
        def body(x, _):
            here = pl.ds(pl.multiple_of(x * (width // 4), 16), width // 4)
            lhs = (stash_at if q == 3 else stash_xt)[here, early:]
            rhs = stash_g[early:] if q == 3 else stash_d[early:, q * width : (q + 1) * width]
            block = grads[q, here] + dot(lhs, rhs)
            for z in range(2):
                for y in range(4):
                    piece = block[(4 * z + y) * share : (4 * z + y + 1) * share]
                    piece = jnp.concatenate(
                        [piece[:, : width // 2], piece[:, width // 2 :]], axis=0
                    ).astype(BF16)
                    if q < 2:
                        parts[q][x, z, y] = piece
                    else:
                        parts[q][y, z, x] = piece
            return 0

        lax.fori_loop(0, 4, body, 0, unroll=4)

    class Ring:
        def __init__(self, base, part, me, forward, backward, relay, direct):
            self.part, self.me, self.relay, self.direct = part, me, relay, direct
            ahead, behind, across = (me + 1) % 4, (me + 3) % 4, (me + 2) % 4
            self.ahead, self.behind = ahead, behind
            self.relay_back = send(base, part.at[across, 0], relay.at[0], backward)
            self.relay_on = send(base + 1, part.at[across, 1], relay.at[1], forward)
            self.own_on = send(base + 2, part.at[ahead, 0], direct.at[0, 0], forward)
            self.own_back = send(base + 3, part.at[behind, 1], direct.at[1, 1], backward)
            self.sum_back = send(base + 4, part.at[behind, 0], direct.at[1, 0], backward)
            self.sum_on = send(base + 5, part.at[ahead, 1], direct.at[0, 1], forward)

        def begin(self):
            self.relay_back.start()
            self.relay_on.start()

        def go_on(self):
            self.own_on.start()
            self.own_back.start()

        def pass_on(self):
            for n, copy, relayed, target in (
                (0, self.sum_back, self.relay_back, self.behind),
                (1, self.sum_on, self.relay_on, self.ahead),
            ):
                relayed.wait_recv()
                total = self.part[target, n].astype(F32) + self.relay[n].astype(F32)
                self.part[target, n] = total.astype(BF16)
                copy.start()

        def arrive(self):
            for copy in (self.own_on, self.own_back, self.sum_back, self.sum_on):
                copy.wait_recv()

        def total(self, z):
            return (
                self.part[self.me, z].astype(F32)
                + self.direct[0, z].astype(F32)
                + self.direct[1, z].astype(F32)
            )

        def close(self):
            for copy in (
                self.relay_back, self.relay_on, self.own_on,
                self.own_back, self.sum_back, self.sum_on,
            ):
                copy.wait_send()

    on_x = (x_at, at(2, 0), at(-2, 0))
    on_y = (col, at(0, 1), at(0, -1))
    outer, inner = [], []
    for q in range(4):
        axes = (on_x, on_y) if q < 2 else (on_y, on_x)
        for rings, name, axis, base in (
            (outer, "part_%d", axes[0], 16),
            (inner, "next_%d", axes[1], 40),
        ):
            rings.append(
                Ring(
                    base + 6 * q,
                    r[name % q],
                    *axis,
                    r["relay_" + name % q],
                    r["direct_" + name % q],
                )
            )

    def turn(q):
        outer[q].arrive()
        for z in range(2):
            total = outer[q].total(z).astype(BF16)
            for n in range(4):
                inner[q].part[n, z] = total[n]
        inner[q].begin()
        inner[q].go_on()

    last_out, last_in, mine = r["last_out"], r["last_in"], r["mine"]
    crossing = [send(64 + q, last_out.at[q], last_in.at[q], at(1 - 2 * z_at, 0)) for q in range(4)]

    def cross(q):
        inner[q].arrive()
        last_out[q] = inner[q].total(1 - z_at).astype(BF16)
        crossing[q].start()
        mine[q] = inner[q].total(z_at)

    def place(k, _):
        left = left_in[pl.ds(pl.multiple_of(16 * k, 16), 16)].astype(F32)
        for n in range(4):
            at_row = 4 * k + n
            tile = left[WIN * (n // 2) : WIN * (n // 2 + 1)]
            before = swap_halves(tile) if n % 2 else tile
            for m in range(pairs):
                here = slice(16 * m, 16 * m + 16)
                both = br[at_row, here].astype(F32)
                lo, hi = both[:WIN], both[WIN:]
                grad = jnp.concatenate(
                    [jnp.where(low, before, lo), jnp.where(low, lo, hi)], axis=0
                )
                r["out_v"][at_row, here] = (xg[1, at_row, here].astype(F32) + grad).astype(BF16)
                before = hi
        return 0

    order = (0, 2, 1, 3)
    for q in order:
        close_grads(q)
        outer[q].begin()
        outer[q].go_on()
    finish(jnp.int32(2 * pairs - 1))
    corner_down.start()
    row_back.start()
    for q in order:
        outer[q].pass_on()
    col_back.wait_recv()
    lax.fori_loop(1, tile_rows // 4, place, 0)
    stores = [
        pltpu.make_async_copy(r["out_v"].at[rows], r["out"].at[rows], r["load_sems"].at[4 + n])
        for n, rows in enumerate((pl.ds(HALF, tile_rows - HALF), pl.ds(0, HALF)))
    ]
    stores[0].start()
    for q in order:
        turn(q)
    corner_down.wait_recv()
    corner_right.start()
    for q in order:
        inner[q].pass_on()
    row_back.wait_recv()
    corner_right.wait_recv()
    lax.fori_loop(0, 1, place, 0)
    stores[1].start()
    for q in order:
        cross(q)
    for q in (0, 2, 1, 3):
        crossing[q].wait_recv()
        total = mine[q] + last_in[q].astype(F32)
        total = jnp.concatenate([total[:share], total[share:]], axis=1)
        if q < 3:
            r["qkv_grad"][:, q * width : (q + 1) * width] = total
        else:
            r["proj_grad"][...] = total

    for array in (0, 1):
        for m in (1, 0):
            row_halo(array, m).wait_send()
    for copy in (col_halo, corner, col_back, corner_down, corner_right, row_back, *crossing):
        copy.wait_send()
    for ring in (*outer, *inner):
        ring.close()
    for store in stores:
        store.wait()


def hand_over(scene_in, qkv_in, proj_in, scene_grad, qkv_grad, proj_grad, a, b, c, come, go):
    step = scene_in.shape[0] // 8
    pieces = [(qkv_in, b, qkv_grad), (proj_in, c, proj_grad)]
    for n in range(8):
        here = pl.ds(n * step, step)
        pieces.append((scene_in.at[here], a.at[here], scene_grad.at[here]))
    loads = [pltpu.make_async_copy(x, y, come.at[n]) for n, (x, y, _) in enumerate(pieces)]
    stores = [pltpu.make_async_copy(y, z, go.at[n]) for n, (_, y, z) in enumerate(pieces)]
    for load in loads:
        load.start()
    for load, store in zip(loads, stores):
        load.wait()
        store.start()
    for store in stores:
        store.wait()


def on_device(scene, cotangent, query_key_value_weight, proj_weight, kept):
    rows, cols, width = scene.shape
    share = width // 32
    piece = (2 * share, width // 2)
    tokens = rows * HALF
    all_tokens = rows * cols
    vmem = {
        "xg": ((2, rows + HALF, cols + 16, width), BF16),
        "br": ((rows + HALF, cols, width), BF16),
        "stash_d": ((all_tokens, 3 * width), BF16),
        "stash_g": ((all_tokens, width), BF16),
        "stash_xt": ((width, all_tokens), BF16),
        "stash_at": ((width, all_tokens), BF16),
        "grads": ((4, width, width), F32),
        "out_v": ((rows, cols, width), BF16),
        "xb": ((BATCH, width), BF16),
        "xh": ((BATCH, width), F32),
        "inv": ((BATCH, 128), F32),
        "qkv": ((BATCH, 3 * width), BF16),
        "dat": ((BATCH, width), BF16),
        "att": ((BATCH, width), BF16),
        "dxh": ((BATCH, width), F32),
        "last": ((WIN, WIN, width), F32),
        "wqkv": ((width, 3 * width), BF16),
        "wp": ((width, width), BF16),
        "wqkv_t": ((3 * width, width), BF16),
        "wp_t": ((width, width), BF16),
        "edge_f": ((2, tokens, width), F32),
        "edge_out": ((2, tokens, width), BF16),
        "edge_in": ((2, tokens, width), BF16),
        "corner_in": ((2, 16, width), BF16),
        "edge_ret": ((tokens, width), BF16),
        "left_in": ((tokens, width), BF16),
        "corner_mid": ((16, width), BF16),
        "last_out": ((4, *piece), BF16),
        "last_in": ((4, *piece), BF16),
        "mine": ((4, *piece), F32),
    }
    for q in range(4):
        vmem["part_%d" % q] = ((4, 2, 4, *piece), BF16)
        vmem["relay_part_%d" % q] = ((2, 4, *piece), BF16)
        vmem["direct_part_%d" % q] = ((2, 2, 4, *piece), BF16)
        vmem["next_%d" % q] = ((4, 2, *piece), BF16)
        vmem["relay_next_%d" % q] = ((2, *piece), BF16)
        vmem["direct_next_%d" % q] = ((2, 2, *piece), BF16)
    sems = {
        "load_sems": pltpu.SemaphoreType.DMA((6,)),
        "send_sems": pltpu.SemaphoreType.DMA((68,)),
        "recv_sems": pltpu.SemaphoreType.DMA((68,)),
    }
    names = (
        ["scene", "cotangent", "wqkv_hbm", "wp_hbm", "kept", "out", "qkv_grad", "proj_grad"]
        + list(vmem)
        + list(sems)
    )
    anywhere = pl.BlockSpec(memory_space=pl.ANY)
    in_vmem = pl.BlockSpec(memory_space=pltpu.VMEM)
    grads = pl.pallas_call(
        functools.partial(kernel, names),
        out_shape=(
            jax.ShapeDtypeStruct((rows, cols, width), BF16),
            jax.ShapeDtypeStruct((share, 3 * width), F32),
            jax.ShapeDtypeStruct((share, width), F32),
        ),
        in_specs=[anywhere] * 4 + [pl.BlockSpec(memory_space=pltpu.SMEM)],
        out_specs=(anywhere, in_vmem, in_vmem),
        scratch_shapes=[pltpu.VMEM(*spec) for spec in vmem.values()] + list(sems.values()),
        compiler_params=pltpu.CompilerParams(
            collective_id=0, has_side_effects=True, vmem_limit_bytes=60 * 1024 * 1024
        ),
    )(scene, cotangent, query_key_value_weight, proj_weight, kept.T)
    return pl.pallas_call(
        hand_over,
        out_shape=tuple(jax.ShapeDtypeStruct(a.shape, a.dtype) for a in grads),
        in_specs=[anywhere] * 3,
        out_specs=(anywhere,) * 3,
        scratch_shapes=[pltpu.VMEM(a.shape, a.dtype) for a in grads]
        + [pltpu.SemaphoreType.DMA((10,)), pltpu.SemaphoreType.DMA((10,))],
    )(*grads)


def solution(mesh):
    return jax.shard_map(
        on_device,
        mesh=mesh,
        in_specs=(
            P(("scene", "row"), "col", None),
            P(("scene", "row"), "col", None),
            P(),
            P(),
            P("scene", None),
        ),
        out_specs=(
            P(("scene", "row"), "col", None),
            P(("scene", "row", "col"), None),
            P(("scene", "row", "col"), None),
        ),
        check_vma=False,
    )
```

```python
import functools

import jax
import jax.numpy as jnp
from jax import lax
from jax.experimental import pallas as pl
from jax.experimental.pallas import tpu as pltpu
from jax.sharding import PartitionSpec as P

HD = 32
WIN = 8
HALF = 4
AREA = 64
PACK = 4
GROUP = PACK * HD
BATCH = 2 * AREA
F32 = jnp.float32
BF16 = jnp.bfloat16
NT = (((1,), (1,)), ((), ()))
TN = (((0,), (0,)), ((), ()))


def dot(a, b, dims=(((1,), (0,)), ((), ()))):
    return lax.dot_general(a, b, dims, preferred_element_type=F32)


def swap_halves(tile):
    return pltpu.roll(tile, HALF, tile.ndim - 2)


def kernel(names, *refs):
    r = dict(zip(names, refs))
    scene, cot = r["scene"], r["cotangent"]
    xg, br, stash_d, stash_g = r["xg"], r["br"], r["stash_d"], r["stash_g"]
    stash_xt, stash_at = r["stash_xt"], r["stash_at"]
    xb_s, xh_s, inv_s, qkv_s, dat_s, att_s = (
        r["xb"], r["xh"], r["inv"], r["qkv"], r["dat"], r["att"],
    )
    wqkv, wp = r["wqkv"], r["wp"]
    tile_rows, tile_cols, width = scene.shape
    groups = width // GROUP
    pairs = tile_cols // 16
    row, col = lax.axis_index("row"), lax.axis_index("col")
    nrow, ncol = lax.axis_size("row"), lax.axis_size("col")
    x_at, z_at = row // 2, row % 2
    myself = row * ncol + col

    def at(drow, dcol):
        return {"row": (row + drow + nrow) % nrow, "col": (col + dcol + ncol) % ncol}

    def send(number, src, dst, device):
        return pltpu.make_async_remote_copy(
            src_ref=src,
            dst_ref=dst,
            send_sem=r["send_sems"].at[number],
            recv_sem=r["recv_sems"].at[number],
            device_id=device,
            device_id_type=pl.DeviceIdType.MESH,
        )

    barrier = pltpu.get_barrier_semaphore()
    partners = [(-1, 0), (1, 0), (0, -1), (0, 1), (2, 0), (-2, 0)]
    for partner in partners:
        pl.semaphore_signal(
            barrier, inc=1, device_id=at(*partner), device_id_type=pl.DeviceIdType.MESH
        )

    own = pl.ds(0, tile_rows)
    loads = [
        pltpu.make_async_copy(src, dst, r["load_sems"].at[k])
        for k, (src, dst) in enumerate(
            [
                (scene, xg.at[0, own, pl.ds(0, tile_cols)]),
                (cot, xg.at[1, own, pl.ds(0, tile_cols)]),
                (r["wqkv_hbm"], wqkv),
                (r["wp_hbm"], wp),
            ]
        )
    ]
    for load in loads:
        load.start()

    def row_halo(array, m):
        src = (scene, cot)[array]
        columns = pl.ds(m * 16, 16)
        return send(
            2 * m + array,
            src.at[pl.ds(0, HALF), columns],
            xg.at[array, pl.ds(tile_rows, HALF), columns],
            at(-1, 0),
        )

    low = lax.broadcasted_iota(jnp.int32, (WIN, width), 0) < HALF

    loads[0].wait()
    loads[1].wait()

    def pack_columns(k, _):
        for array in (0, 1):
            pair = xg[array, pl.ds(2 * k, 2), pl.ds(0, 16)].astype(F32)[:, :WIN]
            tile = jnp.where(low, pair[0], swap_halves(pair[1]))
            r["edge_f"][array, pl.ds(pl.multiple_of(k * WIN, WIN), WIN)] = tile
        return 0

    lax.fori_loop(0, tile_rows // 2, pack_columns, 0)
    r["edge_out"][...] = r["edge_f"][...].astype(BF16)

    edge_in, corner_in = r["edge_in"], r["corner_in"]
    tokens = tile_rows * HALF
    col_halo = send(8, r["edge_out"], edge_in, at(0, -1))
    corner = send(9, edge_in.at[:, pl.ds(0, 16)], corner_in, at(-1, 0))
    pl.semaphore_wait(barrier, len(partners))
    for m in (3, 2):
        for array in (0, 1):
            row_halo(array, m).start()
    col_halo.start()

    def unpack_columns(source, start, first_row, count):
        def body(k, _):
            for array in (0, 1):
                both = source[array, pl.ds(pl.multiple_of(start + k * 16, 16), 16)].astype(F32)
                for n in (0, 1):
                    tile = both[n * WIN : (n + 1) * WIN]
                    for odd in (0, 1):
                        part = swap_halves(tile) if odd else tile
                        whole = jnp.concatenate([part, jnp.zeros_like(part)], axis=0)
                        xg[array, first_row + 4 * k + 2 * n + odd, pl.ds(tile_cols, 16)] = (
                            whole.astype(BF16)
                        )
            return 0

        lax.fori_loop(0, count, body, 0)

    for load in loads[2:]:
        load.wait()
    wqkv_t, wp_t = r["wqkv_t"], r["wp_t"]
    for n in range(3):
        wqkv_t[n * width : (n + 1) * width] = wqkv[:, n * width : (n + 1) * width].T
    wp_t[...] = wp[...].T

    edge_ret, left_in, corner_mid = r["edge_ret"], r["left_in"], r["corner_mid"]
    col_back = send(
        10, edge_ret.at[pl.ds(0, tokens - 16)], left_in.at[pl.ds(16, tokens - 16)], at(0, 1)
    )
    corner_down = send(11, edge_ret.at[pl.ds(tokens - 16, 16)], corner_mid, at(1, 0))
    corner_right = send(12, corner_mid, left_in.at[pl.ds(0, 16)], at(0, 1))
    row_back = send(
        13, br.at[pl.ds(tile_rows, HALF)], br.at[pl.ds(0, HALF)], at(1, 0)
    )

    scale = HD ** (-0.5)
    lane_head = lax.broadcasted_iota(jnp.int32, (AREA, GROUP), 1) // HD
    key_at = lax.broadcasted_iota(jnp.int32, (AREA, PACK * AREA), 0)
    query_at = lax.broadcasted_iota(jnp.int32, (AREA, PACK * AREA), 1) % AREA
    row_differs = jnp.where(key_at // 32 != query_at // 32, 1, 0)
    col_differs = jnp.where((key_at % 8) // 4 != (query_at % 8) // 4, 1, 0)

    def spread(block):
        zero = jnp.zeros_like(block)
        return jnp.concatenate([jnp.where(lane_head == h, block, zero) for h in range(PACK)], axis=0)

    def gather_heads(full):
        total = full[:AREA]
        for h in range(1, PACK):
            total = jnp.where(lane_head == h, full[h * AREA : (h + 1) * AREA], total)
        return total

    grads = r["grads"]
    early = 6 * BATCH

    def gather_early(x, _):
        here = pl.ds(pl.multiple_of(x * (width // 4), 16), width // 4)
        for q in range(4):
            lhs = (stash_at if q == 3 else stash_xt)[here, :early]
            rhs = stash_g[:early] if q == 3 else stash_d[:early, q * width : (q + 1) * width]
            grads[q, here] = dot(lhs, rhs)
        return 0

    def place_of(p):
        i = p // pairs
        return i, p + i * (2 * pairs - 1 - 2 * p)

    def finish(p):
        i, m = place_of(p)
        first = pl.multiple_of(p * BATCH, BATCH)
        here = pl.ds(pl.multiple_of(16 * m, 16), 16)
        r["dxh"][...] = dot(stash_d[pl.ds(first, BATCH)], wqkv_t[...])

        last = []
        for at_row in range(WIN):
            tiles = []
            for w in (0, 1):
                near_row = slice(w * AREA + WIN * at_row, w * AREA + WIN * (at_row + 1))
                grad, normed = r["dxh"][near_row], xh_s[near_row]
                inverse = inv_s[near_row][:, :1]
                tiles.append(
                    inverse
                    * (
                        grad
                        - jnp.mean(grad, axis=-1, keepdims=True)
                        - normed * jnp.mean(grad * normed, axis=-1, keepdims=True)
                    )
                )
            br[HALF + WIN * i + at_row, here] = jnp.concatenate(tiles, axis=0).astype(BF16)
            r["last"][at_row] = tiles[1]

        @pl.when(m == pairs - 1)
        def _():
            last = r["last"][...]
            packed = [
                jnp.where(low, last[2 * n], swap_halves(last[2 * n + 1])) for n in range(WIN // 2)
            ]
            edge_ret[pl.ds(pl.multiple_of(32 * i, 32), 32)] = jnp.concatenate(
                packed, axis=0
            ).astype(BF16)

    def step(p, _):
        i, m = place_of(p)

        @pl.when(p > 0)
        def _():
            finish(p - 1)

        @pl.when(p == 2)
        def _():
            col_halo.wait_recv()
            corner.start()
            unpack_columns(edge_in, 16, HALF, (tile_rows - HALF) // 4)

        @pl.when(p == 4)
        def _():
            for array in (0, 1):
                row_halo(array, 3).wait_send()
            for array in (0, 1):
                row_halo(array, 1).start()
            for array in (0, 1):
                row_halo(array, 3).wait_recv()
            corner.wait_recv()
            unpack_columns(corner_in, 0, tile_rows, 1)

        @pl.when(p == 5)
        def _():
            col_back.start()
            for array in (0, 1):
                row_halo(array, 2).wait_send()
            for array in (0, 1):
                row_halo(array, 0).start()
            for array in (0, 1):
                row_halo(array, 2).wait_recv()

        @pl.when(p == 6)
        def _():
            lax.fori_loop(0, 4, gather_early, 0)
            for array in (0, 1):
                row_halo(array, 1).wait_recv()

        @pl.when(p == 7)
        def _():
            for array in (0, 1):
                row_halo(array, 0).wait_recv()

        first = pl.multiple_of(p * BATCH, BATCH)
        here = pl.ds(pl.multiple_of(16 * m, 16), 16)
        following = pl.ds(pl.multiple_of(16 * m + 16, 16), 16)
        keep = [r["kept"][WIN * i + 2 * m + w, myself].astype(F32) for w in range(2)]
        for rows in range(4):
            top = pl.ds(WIN * i + HALF + 2 * rows, 2)
            for array in (0, 1):
                t0 = xg[array, top, here].astype(F32)
                t1 = xg[array, top, following].astype(F32)
                lo, hi, nx = t0[:, :WIN], t0[:, WIN:], t1[:, :WIN]
                for w, (a, c) in enumerate(((lo, hi), (hi, nx))):
                    tile = jnp.where(low, c, a).reshape(2 * WIN, width)
                    start = w * AREA + 16 * rows
                    if array == 0:
                        mean = jnp.mean(tile, axis=-1, keepdims=True)
                        centred = tile - mean
                        inverse = lax.rsqrt(
                            jnp.mean(centred * centred, axis=-1, keepdims=True) + 1e-05
                        )
                        normed = centred * inverse
                        xh_s[start : start + 16] = normed
                        xb_s[start : start + 16] = normed.astype(BF16)
                        inv_s[start : start + 16] = jnp.broadcast_to(inverse, (16, 128))
                    else:
                        stash_g[pl.ds(pl.multiple_of(first + start, 16), 16)] = (
                            tile * keep[w]
                        ).astype(BF16)

        xb = xb_s[...]
        stash_xt[:, pl.ds(first, BATCH)] = xb.T
        for n in range(3):
            qkv_s[:, n * width : (n + 1) * width] = dot(
                xb, wqkv[:, n * width : (n + 1) * width]
            ).astype(BF16)
        dat_s[...] = dot(stash_g[pl.ds(first, BATCH)], wp_t[...]).astype(BF16)

        last_row = jnp.where(row == nrow - 1, i, 0)
        last_col = jnp.where(col == ncol - 1, m // (pairs - 1), 0)
        biases = [
            jnp.where(row_differs * last_row + col_differs * lc > 0, -100.0, 0.0)
            for lc in (0, last_col)
        ]

        def part(n, g):
            return slice(n * width + g * GROUP, n * width + (g + 1) * GROUP)

        units = [(w, g) for w in range(2) for g in range(groups)]
        near = [slice(w * AREA, (w + 1) * AREA) for w in range(2)]
        far = [pl.ds(pl.multiple_of(first + w * AREA, AREA), AREA) for w in range(2)]
        q, k, v = [[qkv_s[near[w], part(n, g)] for w, g in units] for n in range(3)]
        spread_q = [spread(block) for block in q]
        spread_d = [spread(dat_s[near[w], part(0, g)]) for w, g in units]
        scores = [
            dot(a, c, NT) * scale + biases[w] for (w, _), a, c in zip(units, k, spread_q)
        ]
        d_p = [dot(a, c, NT) for a, c in zip(v, spread_d)]
        expo = [jnp.exp(a - jnp.max(a, axis=0, keepdims=True)) for a in scores]
        probs = [a * (1.0 / jnp.sum(a, axis=0, keepdims=True)) for a in expo]
        pb = [a.astype(BF16) for a in probs]
        d_s = [
            (a * (c - jnp.sum(a * c, axis=0, keepdims=True)) * scale).astype(BF16)
            for a, c in zip(probs, d_p)
        ]
        attended = [dot(a, c, TN) for a, c in zip(pb, v)]
        d_v = [dot(a, c) for a, c in zip(pb, spread_d)]
        d_q = [dot(a, c, TN) for a, c in zip(d_s, k)]
        d_k = [dot(a, c) for a, c in zip(d_s, spread_q)]
        for n, (w, g) in enumerate(units):
            att_s[near[w], part(0, g)] = gather_heads(attended[n]).astype(BF16)
            stash_d[far[w], part(0, g)] = gather_heads(d_q[n]).astype(BF16)
            stash_d[far[w], part(1, g)] = d_k[n].astype(BF16)
            stash_d[far[w], part(2, g)] = d_v[n].astype(BF16)

        stash_at[:, pl.ds(first, BATCH)] = att_s[...].T
        return 0

    lax.fori_loop(0, 2 * pairs, step, 0)

    share = width // (nrow * ncol)
    parts = [r["part_%d" % q] for q in range(4)]

    def close_grads(q):
        def body(x, _):
            here = pl.ds(pl.multiple_of(x * (width // 4), 16), width // 4)
            lhs = (stash_at if q == 3 else stash_xt)[here, early:]
            rhs = stash_g[early:] if q == 3 else stash_d[early:, q * width : (q + 1) * width]
            block = grads[q, here] + dot(lhs, rhs)
            for z in range(2):
                for y in range(4):
                    piece = block[(4 * z + y) * share : (4 * z + y + 1) * share]
                    piece = jnp.concatenate(
                        [piece[:, : width // 2], piece[:, width // 2 :]], axis=0
                    ).astype(BF16)
                    if q < 2:
                        parts[q][x, z, y] = piece
                    else:
                        parts[q][y, z, x] = piece
            return 0

        for n in range(4):
            body((x_at + 2 + n) % 4 if q < 2 else n, 0)
            if q < 2 and n == 0:
                outer[q].begin()
        if q >= 2:
            outer[q].begin()

    class Ring:
        def __init__(self, base, part, me, forward, backward, relay, direct):
            self.part, self.me, self.relay, self.direct = part, me, relay, direct
            ahead, behind, across = (me + 1) % 4, (me + 3) % 4, (me + 2) % 4
            self.ahead, self.behind = ahead, behind
            self.relay_back = send(base, part.at[across, 0], relay.at[0], backward)
            self.relay_on = send(base + 1, part.at[across, 1], relay.at[1], forward)
            self.own_on = send(base + 2, part.at[ahead, 0], direct.at[0, 0], forward)
            self.own_back = send(base + 3, part.at[behind, 1], direct.at[1, 1], backward)
            self.sum_back = send(base + 4, part.at[behind, 0], direct.at[1, 0], backward)
            self.sum_on = send(base + 5, part.at[ahead, 1], direct.at[0, 1], forward)

        def begin(self):
            self.relay_back.start()
            self.relay_on.start()

        def go_on(self):
            self.own_on.start()
            self.own_back.start()

        def pass_on(self):
            for n, copy, relayed, target in (
                (0, self.sum_back, self.relay_back, self.behind),
                (1, self.sum_on, self.relay_on, self.ahead),
            ):
                relayed.wait_recv()
                total = self.part[target, n].astype(F32) + self.relay[n].astype(F32)
                self.part[target, n] = total.astype(BF16)
                copy.start()

        def arrive(self):
            for copy in (self.own_on, self.own_back, self.sum_back, self.sum_on):
                copy.wait_recv()

        def total(self, z):
            return (
                self.part[self.me, z].astype(F32)
                + self.direct[0, z].astype(F32)
                + self.direct[1, z].astype(F32)
            )

        def close(self):
            for copy in (
                self.relay_back, self.relay_on, self.own_on,
                self.own_back, self.sum_back, self.sum_on,
            ):
                copy.wait_send()

    on_x = (x_at, at(2, 0), at(-2, 0))
    on_y = (col, at(0, 1), at(0, -1))
    outer, inner = [], []
    for q in range(4):
        axes = (on_x, on_y) if q < 2 else (on_y, on_x)
        for rings, name, axis, base in (
            (outer, "part_%d", axes[0], 16),
            (inner, "next_%d", axes[1], 40),
        ):
            rings.append(
                Ring(
                    base + 6 * q,
                    r[name % q],
                    *axis,
                    r["relay_" + name % q],
                    r["direct_" + name % q],
                )
            )

    def turn(q):
        outer[q].arrive()
        for z in range(2):
            total = outer[q].total(z).astype(BF16)
            for n in range(4):
                inner[q].part[n, z] = total[n]
        inner[q].begin()
        inner[q].go_on()

    last_out, last_in, mine = r["last_out"], r["last_in"], r["mine"]
    crossing = [send(64 + q, last_out.at[q], last_in.at[q], at(1 - 2 * z_at, 0)) for q in range(4)]

    def cross(q):
        inner[q].arrive()
        last_out[q] = inner[q].total(1 - z_at).astype(BF16)
        crossing[q].start()
        mine[q] = inner[q].total(z_at)

    def place(k, _):
        left = left_in[pl.ds(pl.multiple_of(16 * k, 16), 16)].astype(F32)
        for n in range(4):
            at_row = 4 * k + n
            tile = left[WIN * (n // 2) : WIN * (n // 2 + 1)]
            before = swap_halves(tile) if n % 2 else tile
            for m in range(pairs):
                here = slice(16 * m, 16 * m + 16)
                both = br[at_row, here].astype(F32)
                lo, hi = both[:WIN], both[WIN:]
                grad = jnp.concatenate(
                    [jnp.where(low, before, lo), jnp.where(low, lo, hi)], axis=0
                )
                r["out_v"][at_row, here] = (xg[1, at_row, here].astype(F32) + grad).astype(BF16)
                before = hi
        return 0

    order = (0, 2, 1, 3)
    for q in order:
        close_grads(q)
        outer[q].go_on()
    finish(jnp.int32(2 * pairs - 1))
    corner_down.start()
    row_back.start()
    for q in order:
        outer[q].pass_on()
    col_back.wait_recv()
    lax.fori_loop(1, tile_rows // 4, place, 0)
    stores = [
        pltpu.make_async_copy(r["out_v"].at[rows], r["out"].at[rows], r["load_sems"].at[4 + n])
        for n, rows in enumerate((pl.ds(HALF, tile_rows - HALF), pl.ds(0, HALF)))
    ]
    stores[0].start()
    for q in order:
        turn(q)
    corner_down.wait_recv()
    corner_right.start()
    for q in order:
        inner[q].pass_on()
    row_back.wait_recv()
    corner_right.wait_recv()
    lax.fori_loop(0, 1, place, 0)
    stores[1].start()
    for q in order:
        cross(q)
    for q in (0, 2, 1, 3):
        crossing[q].wait_recv()
        total = mine[q] + last_in[q].astype(F32)
        total = jnp.concatenate([total[:share], total[share:]], axis=1)
        if q < 3:
            r["qkv_grad"][:, q * width : (q + 1) * width] = total
        else:
            r["proj_grad"][...] = total

    for array in (0, 1):
        for m in (1, 0):
            row_halo(array, m).wait_send()
    for copy in (col_halo, corner, col_back, corner_down, corner_right, row_back, *crossing):
        copy.wait_send()
    for ring in (*outer, *inner):
        ring.close()
    for store in stores:
        store.wait()


def hand_over(scene_in, qkv_in, proj_in, scene_grad, qkv_grad, proj_grad, a, b, c, come, go):
    step = scene_in.shape[0] // 8
    pieces = []
    for n in range(8):
        here = pl.ds(n * step, step)
        pieces.append((scene_in.at[here], a.at[here], scene_grad.at[here]))
    pieces += [(qkv_in, b, qkv_grad), (proj_in, c, proj_grad)]
    loads = [pltpu.make_async_copy(x, y, come.at[n]) for n, (x, y, _) in enumerate(pieces)]
    stores = [pltpu.make_async_copy(y, z, go.at[n]) for n, (_, y, z) in enumerate(pieces)]
    for load in loads:
        load.start()
    for load, store in zip(loads, stores):
        load.wait()
        store.start()
    for store in stores:
        store.wait()


def on_device(scene, cotangent, query_key_value_weight, proj_weight, kept):
    rows, cols, width = scene.shape
    share = width // 32
    piece = (2 * share, width // 2)
    tokens = rows * HALF
    all_tokens = rows * cols
    vmem = {
        "xg": ((2, rows + HALF, cols + 16, width), BF16),
        "br": ((rows + HALF, cols, width), BF16),
        "stash_d": ((all_tokens, 3 * width), BF16),
        "stash_g": ((all_tokens, width), BF16),
        "stash_xt": ((width, all_tokens), BF16),
        "stash_at": ((width, all_tokens), BF16),
        "grads": ((4, width, width), F32),
        "out_v": ((rows, cols, width), BF16),
        "xb": ((BATCH, width), BF16),
        "xh": ((BATCH, width), F32),
        "inv": ((BATCH, 128), F32),
        "qkv": ((BATCH, 3 * width), BF16),
        "dat": ((BATCH, width), BF16),
        "att": ((BATCH, width), BF16),
        "dxh": ((BATCH, width), F32),
        "last": ((WIN, WIN, width), F32),
        "wqkv": ((width, 3 * width), BF16),
        "wp": ((width, width), BF16),
        "wqkv_t": ((3 * width, width), BF16),
        "wp_t": ((width, width), BF16),
        "edge_f": ((2, tokens, width), F32),
        "edge_out": ((2, tokens, width), BF16),
        "edge_in": ((2, tokens, width), BF16),
        "corner_in": ((2, 16, width), BF16),
        "edge_ret": ((tokens, width), BF16),
        "left_in": ((tokens, width), BF16),
        "corner_mid": ((16, width), BF16),
        "last_out": ((4, *piece), BF16),
        "last_in": ((4, *piece), BF16),
        "mine": ((4, *piece), F32),
    }
    for q in range(4):
        vmem["part_%d" % q] = ((4, 2, 4, *piece), BF16)
        vmem["relay_part_%d" % q] = ((2, 4, *piece), BF16)
        vmem["direct_part_%d" % q] = ((2, 2, 4, *piece), BF16)
        vmem["next_%d" % q] = ((4, 2, *piece), BF16)
        vmem["relay_next_%d" % q] = ((2, *piece), BF16)
        vmem["direct_next_%d" % q] = ((2, 2, *piece), BF16)
    sems = {
        "load_sems": pltpu.SemaphoreType.DMA((6,)),
        "send_sems": pltpu.SemaphoreType.DMA((68,)),
        "recv_sems": pltpu.SemaphoreType.DMA((68,)),
    }
    names = (
        ["scene", "cotangent", "wqkv_hbm", "wp_hbm", "kept", "out", "qkv_grad", "proj_grad"]
        + list(vmem)
        + list(sems)
    )
    anywhere = pl.BlockSpec(memory_space=pl.ANY)
    in_vmem = pl.BlockSpec(memory_space=pltpu.VMEM)
    grads = pl.pallas_call(
        functools.partial(kernel, names),
        out_shape=(
            jax.ShapeDtypeStruct((rows, cols, width), BF16),
            jax.ShapeDtypeStruct((share, 3 * width), F32),
            jax.ShapeDtypeStruct((share, width), F32),
        ),
        in_specs=[anywhere] * 4 + [pl.BlockSpec(memory_space=pltpu.SMEM)],
        out_specs=(anywhere, in_vmem, in_vmem),
        scratch_shapes=[pltpu.VMEM(*spec) for spec in vmem.values()] + list(sems.values()),
        compiler_params=pltpu.CompilerParams(
            collective_id=0, has_side_effects=True, vmem_limit_bytes=60 * 1024 * 1024
        ),
    )(scene, cotangent, query_key_value_weight, proj_weight, kept.T)
    return pl.pallas_call(
        hand_over,
        out_shape=tuple(jax.ShapeDtypeStruct(a.shape, a.dtype) for a in grads),
        in_specs=[anywhere] * 3,
        out_specs=(anywhere,) * 3,
        scratch_shapes=[pltpu.VMEM(a.shape, a.dtype) for a in grads]
        + [pltpu.SemaphoreType.DMA((10,)), pltpu.SemaphoreType.DMA((10,))],
    )(*grads)


def solution(mesh):
    return jax.shard_map(
        on_device,
        mesh=mesh,
        in_specs=(
            P(("scene", "row"), "col", None),
            P(("scene", "row"), "col", None),
            P(),
            P(),
            P("scene", None),
        ),
        out_specs=(
            P(("scene", "row"), "col", None),
            P(("scene", "row", "col"), None),
            P(("scene", "row", "col"), None),
        ),
        check_vma=False,
    )
```
